32 devices in a mesh: blk: 8 (over z, x), mp: 4 (over y, core).
Axes of the slice: x: 2, y: 2, z: 4, core: 2. Of those that a mesh axis runs over, the one named last changes fastest.
Arguments:
- tokens_in: bfloat16 [2048, 2048], P('blk'), may hold values from -17 to 17
- w_qkv: bfloat16 [3, 2048, 2048], P(None, None, 'mp'), may hold values from -0.125 to 0.125
- w_out: bfloat16 [2048, 2048], P('mp'), may hold values from -0.125 to 0.125
- grad_y: bfloat16 [2048, 2048], P('blk'), may hold values from -6 to 6
- block_cols: int32 [16, 2], replicated, may hold values from 0 to 15, as said below
- block_count: int32 [16], replicated, may hold values from 1 to 2, as said below
Outputs:
- grad_x: bfloat16 [2048, 2048], P('blk', 'mp')
- grad_qkv: bfloat16 [3, 2048, 2048], P(None, 'blk', 'mp')
- grad_out: bfloat16 [2048, 2048], P('mp', 'blk')
The draws below stay inside these ranges and needn't reach their ends.
Inputs may be any that keep to these rules, and one draw needn't show every extreme that they name: `block_cols`: slot 0 of row r is r itself; the first block_count[r] slots of a row are distinct blocks; later slots repeat r. `block_count`: some rows use all 2 slots.
All inputs are finite; a program needn't handle non-finite values.
Results may differ from the reference program's by a relative error of at most 0.02.
Values may be sent and summed in bfloat16 or wider, within the bound.
No kernel may reach another device: no remote copies, remote signals or barrier semaphores. Data moves between devices by JAX's collectives and lax.ppermute only.
A program may use at most 64 MiB of HBM per device.

```python
import math
import jax
import jax.numpy as jnp
from jax import lax

D = 2048
HEADS = 16
HEAD = 128
BLOCK = 128
TOK_DEV = 256
TOKENS = 2048
NB = 16
MAXB = 2


def draw_tokens_in(key, part):
    return jnp.clip(jax.random.normal(key, (TOKENS, D), jnp.float32), -6.0, 6.0).astype(jnp.bfloat16)


def visibility_draw(key):
    key = jax.random.fold_in(key, 7)
    key_perm, key_busy, key_light = jax.random.split(key, 3)
    row_ids = jnp.arange(NB, dtype=jnp.int32)
    row_keys = jax.random.split(key_perm, NB)
    shuffled = jax.vmap(lambda row_key: jax.random.permutation(row_key, NB - 1))(row_keys).astype(jnp.int32)
    other_cols = (row_ids[:, None] + 1 + shuffled[:, :MAXB - 1]) % NB
    col_table = jnp.concatenate([row_ids[:, None], other_cols], axis=1)
    busy_start = jax.random.randint(key_busy, (), 0, NB)
    busy_rows = (row_ids - busy_start) % NB < max(1, NB // 4)
    light_count = jax.random.randint(key_light, (NB,), 1, max(2, MAXB // 4) + 1)
    live_count = jnp.where(busy_rows, MAXB, light_count).astype(jnp.int32)
    in_use = jnp.arange(MAXB, dtype=jnp.int32)[None, :] < live_count[:, None]
    col_table = jnp.where(in_use, col_table, row_ids[:, None]).astype(jnp.int32)
    return (col_table, live_count)


def draw_block_cols(key, part):
    return visibility_draw(key)[0]


def draw_block_count(key, part):
    return visibility_draw(key)[1]


def block_scale(own_key, extent, cuts, smallest, top_value):
    def one(axis_at, parts):
        draws = jax.random.uniform(jax.random.fold_in(jax.random.fold_in(own_key, 6), axis_at), (parts,), jnp.float32, smallest / len(cuts), top_value / len(cuts))
        return jnp.repeat(jnp.exp(draws), extent[axis_at] // parts).reshape((-1,) + (1,) * (len(extent) - axis_at - 1))

    loudness = one(*cuts[0])
    for cut in cuts[1:]:
        loudness = loudness * one(*cut)
    return loudness


def noise(key, extent, deviation, most, pieces=(), kind=jnp.bfloat16):
    drawn = jax.random.normal(key, extent, jnp.float32) * deviation
    if len(pieces) > 0:
        drawn = block_scale(key, extent, pieces, -0.22, 0.18) * drawn
    return jnp.clip(drawn, min=-most, max=most).astype(kind)


def setup_inputs(seed: int = 0) -> dict:
    arg_keys = jax.random.split(jax.random.key(seed), 7)
    tokens_in = draw_tokens_in(jax.random.fold_in(arg_keys[6], 71), 0)
    w_qkv = noise(arg_keys[1], (3, D, D), D ** -0.5, 0.125, ((2, 4),))
    w_out = noise(arg_keys[2], (D, D), D ** -0.5, 0.125, ((0, 4),))
    grad_y = noise(arg_keys[3], (TOKENS, D), 1.0, 6.0, ((0, 8),))
    block_cols = draw_block_cols(jax.random.fold_in(arg_keys[6], 71), 0)
    block_count = draw_block_count(jax.random.fold_in(arg_keys[6], 71), 0)
    return dict(tokens_in=tokens_in, w_qkv=w_qkv, w_out=w_out, grad_y=grad_y, block_cols=block_cols, block_count=block_count)


NEG_FILL = -1e+30

def block_visibility(block_cols, block_count):
    block_total = block_cols.shape[0]
    slot_ids = jnp.arange(block_cols.shape[1], dtype=jnp.int32)[None, :]
    in_use = slot_ids < block_count[:, None]
    target = jnp.arange(block_total, dtype=jnp.int32)[None, None, :]
    return jnp.any((block_cols[:, :, None] == target) & in_use[:, :, None], axis=1)

def reference(tokens_in, w_qkv, w_out, grad_y, block_cols, block_count):
    score_scale = 1.0 / math.sqrt(HEAD)
    visible = block_visibility(block_cols, block_count)
    tok_block = jnp.arange(TOKENS, dtype=jnp.int32) // BLOCK
    key_visible = jnp.take(visible, tok_block, axis=1)

    def split_heads(flat_rows):
        return flat_rows.reshape(TOKENS, HEADS, HEAD).transpose(1, 0, 2)

    def merge_heads(head_rows):
        return head_rows.transpose(1, 0, 2).reshape(TOKENS, D)

    def project(weight):
        return jnp.dot(tokens_in, weight, preferred_element_type=jnp.float32).astype(jnp.bfloat16)
    queries = split_heads(project(w_qkv[0]))
    keys = split_heads(project(w_qkv[1]))
    values = split_heads(project(w_qkv[2]))
    grad_heads = split_heads(jnp.dot(grad_y, w_out.T, preferred_element_type=jnp.float32).astype(jnp.bfloat16))
    row_blocks = TOKENS // TOK_DEV
    block_ids = jnp.arange(row_blocks, dtype=jnp.int32)

    def row_mask(q_start):
        rows_here = (q_start + jnp.arange(TOK_DEV, dtype=jnp.int32)) // BLOCK
        return jnp.take(key_visible, rows_here, axis=0)

    def forward_head(operands):
        q_head, k_head, v_head = operands

        def one_block(block_id):
            q_start = (block_id * TOK_DEV).astype(jnp.int32)
            q_part = lax.dynamic_slice_in_dim(q_head, q_start, TOK_DEV, 0)
            scores = jnp.where(row_mask(q_start), jnp.dot(q_part, k_head.T, preferred_element_type=jnp.float32) * score_scale, NEG_FILL)
            row_top = lax.optimization_barrier(jnp.max(scores, axis=1, keepdims=True))
            log_sum = row_top + jnp.log(lax.optimization_barrier(jnp.sum(jnp.exp(scores - row_top), axis=1, keepdims=True)))
            weights = jnp.exp(scores - log_sum).astype(jnp.bfloat16)
            return (jnp.dot(weights, v_head, preferred_element_type=jnp.float32).astype(jnp.bfloat16), log_sum[:, 0])
        outputs, log_sums = lax.map(one_block, block_ids)
        return (outputs.reshape(TOKENS, HEAD), log_sums.reshape(TOKENS))
    attended, log_sums = lax.map(forward_head, (queries, keys, values))
    row_delta = lax.optimization_barrier(jnp.sum(attended.astype(jnp.float32) * grad_heads.astype(jnp.float32), axis=2))

    def backward_head(operands):
        q_head, k_head, v_head, g_head, lse_head, delta_head = operands

        def one_block(carried, block_id):
            dk_acc, dv_acc = carried
            q_start = (block_id * TOK_DEV).astype(jnp.int32)
            q_part = lax.dynamic_slice_in_dim(q_head, q_start, TOK_DEV, 0)
            g_part = lax.dynamic_slice_in_dim(g_head, q_start, TOK_DEV, 0)
            lse_part = lax.dynamic_slice_in_dim(lse_head, q_start, TOK_DEV, 0)
            delta_part = lax.dynamic_slice_in_dim(delta_head, q_start, TOK_DEV, 0)
            scores = jnp.where(row_mask(q_start), jnp.dot(q_part, k_head.T, preferred_element_type=jnp.float32) * score_scale, NEG_FILL)
            prob_rows = jnp.exp(scores - lse_part[:, None])
            dv_acc = dv_acc + jnp.dot(prob_rows.astype(jnp.bfloat16).T, g_part, preferred_element_type=jnp.float32)
            dprobs = jnp.dot(g_part, v_head.T, preferred_element_type=jnp.float32)
            dscores = (prob_rows * (dprobs - delta_part[:, None])).astype(jnp.bfloat16)
            dq_part = (jnp.dot(dscores, k_head, preferred_element_type=jnp.float32) * score_scale).astype(jnp.bfloat16)
            dk_acc = dk_acc + jnp.dot(dscores.T, q_part, preferred_element_type=jnp.float32)
            return ((dk_acc, dv_acc), dq_part)
        zero_tile = jnp.zeros((TOKENS, HEAD), jnp.float32)
        (dk_acc, dv_acc), dq_parts = lax.scan(one_block, (zero_tile, zero_tile), block_ids)
        return (dq_parts.reshape(TOKENS, HEAD), (dk_acc * score_scale).astype(jnp.bfloat16), dv_acc.astype(jnp.bfloat16))
    grad_q, grad_k, grad_v = lax.map(backward_head, (queries, keys, values, grad_heads, log_sums, row_delta))
    grad_q, grad_k, grad_v = (merge_heads(grad_q), merge_heads(grad_k), merge_heads(grad_v))
    attended_flat = merge_heads(attended)
    grad_x = (jnp.dot(grad_q, w_qkv[0].T, preferred_element_type=jnp.float32) + jnp.dot(grad_k, w_qkv[1].T, preferred_element_type=jnp.float32) + jnp.dot(grad_v, w_qkv[2].T, preferred_element_type=jnp.float32)).astype(jnp.bfloat16)
    grad_qkv = jnp.stack([jnp.dot(tokens_in.T, grad_q, preferred_element_type=jnp.float32), jnp.dot(tokens_in.T, grad_k, preferred_element_type=jnp.float32), jnp.dot(tokens_in.T, grad_v, preferred_element_type=jnp.float32)]).astype(jnp.bfloat16)
    grad_out = jnp.dot(attended_flat.T, grad_y, preferred_element_type=jnp.float32).astype(jnp.bfloat16)
    return (grad_x, grad_qkv, grad_out)
```

```python
import functools
import math

import jax
import jax.numpy as jnp
from jax import lax
from jax.experimental import pallas as pl
from jax.experimental.pallas import tpu as pltpu
from jax.sharding import Mesh
from jax.sharding import PartitionSpec as P

HEAD = 128
BLOCK = 128
NEG_FILL = -1e30
BF16 = jnp.bfloat16
F32 = jnp.float32


def dot(a, b, dims):
    return lax.dot_general(a, b, (dims, ((), ())), preferred_element_type=F32)


def attention_kernel(cols_ref, count_ref, qkv_ref, g_ref, grads_ref, att_ref, dk_ref, dv_ref):
    row_blocks, slots = cols_ref.shape
    heads = g_ref.shape[1] // HEAD
    scale = 1.0 / math.sqrt(HEAD)
    dk_ref[...] = jnp.zeros_like(dk_ref)
    dv_ref[...] = jnp.zeros_like(dv_ref)

    def row(r, carry):
        rows = pl.ds(pl.multiple_of(r * BLOCK, BLOCK), BLOCK)
        at = [pl.ds(pl.multiple_of(cols_ref[r, s] * BLOCK, BLOCK), BLOCK) for s in range(slots)]
        live = count_ref[r]
        for h in range(heads):
            lanes = slice(h * HEAD, (h + 1) * HEAD)
            q = qkv_ref[0, rows, lanes]
            g = g_ref[rows, lanes]
            k = jnp.concatenate([qkv_ref[1, a, lanes] for a in at], axis=0)
            v = jnp.concatenate([qkv_ref[2, a, lanes] for a in at], axis=0)
            s = dot(k, q, ((1,), (1,))) * scale
            slot_of = lax.broadcasted_iota(jnp.int32, s.shape, 0) // BLOCK
            s = jnp.where(slot_of < live, s, NEG_FILL)
            e = jnp.exp(s - jnp.max(s, axis=0, keepdims=True))
            p = e * (1.0 / jnp.sum(e, axis=0, keepdims=True))
            p16 = p.astype(BF16)
            att_ref[rows, lanes] = dot(p16, v, ((0,), (0,))).astype(BF16)
            dp = dot(v, g, ((1,), (1,)))
            delta = jnp.sum(p * dp, axis=0, keepdims=True)
            ds16 = (p * (dp - delta)).astype(BF16)
            grads_ref[0, rows, lanes] = (dot(ds16, k, ((0,), (0,))) * scale).astype(BF16)
            dk = dot(ds16, q, ((1,), (0,)))
            dv = dot(p16, g, ((1,), (0,)))
            for i, a in enumerate(at):
                part = slice(i * BLOCK, (i + 1) * BLOCK)
                dk_ref[a, lanes] += dk[part]
                dv_ref[a, lanes] += dv[part]
        return carry

    lax.fori_loop(0, row_blocks, row, 0)
    grads_ref[1] = (dk_ref[...] * scale).astype(BF16)
    grads_ref[2] = dv_ref[...].astype(BF16)


def attention(cols, count, qkv, g):
    tokens, width = g.shape
    whole = pl.BlockSpec(memory_space=pltpu.VMEM)
    table = pl.BlockSpec(memory_space=pltpu.SMEM)
    return pl.pallas_call(
        attention_kernel,
        out_shape=(
            jax.ShapeDtypeStruct((3, tokens, width), BF16),
            jax.ShapeDtypeStruct((tokens, width), BF16),
        ),
        in_specs=[table, table, whole, whole],
        out_specs=(whole, whole),
        scratch_shapes=[pltpu.VMEM((tokens, width), F32), pltpu.VMEM((tokens, width), F32)],
        compiler_params=pltpu.CompilerParams(vmem_limit_bytes=48 * 2**20),
        name="attention",
    )(cols, count, qkv, g)


def local(sizes, tokens_in, w_qkv, w_out, grad_y, block_cols, block_count):
    nz, nx, ny, nc = sizes
    chunks, pieces = nz * nx, ny * nc
    tok, width = tokens_in.shape
    piece = tok // pieces
    out_cols = width // chunks
    blocks = tok // BLOCK
    chunk = lax.axis_index("z") * nx + lax.axis_index("x")
    quarter = lax.axis_index("y") * nc + lax.axis_index("c")
    quarter_block = quarter * blocks // pieces

    def swap(a, axis, k):
        n = math.prod(mesh_size[i] for i in axis)
        return lax.ppermute(a, axis, [(i, i ^ k) for i in range(n)])

    mesh_size = dict(z=nz, x=nx, y=ny, c=nc)

    def my_piece(a, k):
        return lax.dynamic_slice_in_dim(a, (quarter ^ k) * piece, piece, 0)

    def spread(parts):
        by_y = [[p] + [swap(p, "y", k) for k in range(1, ny)] for p in parts]
        whole = []
        for ys in by_y:
            mine = jnp.concatenate(ys, axis=0)
            cs = [mine] + [swap(mine, "c", j) for j in range(1, nc)]
            whole.append(
                jnp.concatenate(
                    [cs[j][k * piece : (k + 1) * piece] for k in range(ny) for j in range(nc)], axis=0
                )
            )
        return whole

    own = my_piece(tokens_in, 0)
    along_z = [own] + [swap(own, "z", k) for k in range(1, nz)]
    along_x = [p if j == 0 else swap(p, "x", j) for p in along_z for j in range(nx)]
    all_tokens = [tokens_in] + spread(along_x[1:])

    g_own = dot(grad_y, w_out, ((1,), (1,))).astype(BF16)
    g_sent = jnp.concatenate([my_piece(g_own, k) for k in range(pieces)], axis=0)
    g_z = [g_sent] + [swap(g_sent, "z", k) for k in range(1, nz)]
    g_x = [p if j == 0 else swap(p, "x", j) for p in g_z for j in range(nx)]
    g_all = jnp.concatenate([g_own] + g_x[1:], axis=0)

    y_mine = my_piece(grad_y, 0)

    def columns(a, k):
        return lax.dynamic_slice_in_dim(a, (chunk ^ k) * out_cols, out_cols, 1)

    y_parts = [swap(columns(y_mine, k), ("z", "x"), k) for k in range(1, chunks)]
    y_rows = jnp.stack(y_parts)
    y_by_y = jnp.stack([y_rows] + [swap(y_rows, "y", k) for k in range(1, ny)], axis=1)
    y_by_c = jnp.stack([y_by_y] + [swap(y_by_y, "c", j) for j in range(1, nc)], axis=2)
    y_all = jnp.concatenate([columns(grad_y, 0), y_by_c.reshape((chunks - 1) * tok, out_cols)], axis=0)

    qkv = jnp.concatenate(
        [
            jnp.einsum("td,cde->cte", t, w_qkv, preferred_element_type=F32).astype(BF16)
            for t in all_tokens
        ],
        axis=1,
    )

    place = jnp.arange(chunks * blocks, dtype=jnp.int32)

    def flip(held_chunk):
        return jnp.where(held_chunk == 0, 0, quarter_block)

    held = place // blocks
    block_at = (held ^ chunk) * blocks + ((place % blocks) ^ flip(held))
    pick = block_at[:, None] == place[None, :]
    cols = jnp.sum(jnp.where(pick[:, :, None], block_cols[None], 0), axis=1)
    count = jnp.sum(jnp.where(pick, block_count[None], 0), axis=1)
    cols_held = (cols // blocks) ^ chunk
    cols = cols_held * blocks + ((cols % blocks) ^ flip(cols_held))

    grads, att = attention(cols, count, qkv, g_all)

    dx = jnp.einsum("cte,cde->td", grads[:, :tok], w_qkv, preferred_element_type=F32)
    dx = dx.reshape(tok, ny, nc, width // pieces)
    y, c = lax.axis_index("y"), lax.axis_index("c")

    def at_c(k):
        return lax.dynamic_index_in_dim(dx, c ^ k, 2, keepdims=False)

    half = at_c(0)
    for k in range(1, nc):
        half = half + swap(at_c(k).astype(BF16), "c", k).astype(F32)

    def at_y(k):
        return lax.dynamic_index_in_dim(half, y ^ k, 1, keepdims=False)

    grad_x = at_y(0)
    for k in range(1, ny):
        grad_x = grad_x + swap(at_y(k).astype(BF16), "y", k).astype(F32)

    t_cols = jnp.concatenate([columns(t, 0) for t in all_tokens], axis=0)
    grad_qkv = jnp.einsum("td,cte->cde", t_cols, grads, preferred_element_type=F32)
    grad_out = dot(att, y_all, ((0,), (0,)))
    return (grad_x.astype(BF16), grad_qkv.astype(BF16), grad_out.astype(BF16))


def solution(mesh):
    chunks, pieces = mesh.shape["blk"], mesh.shape["mp"]
    sizes = (chunks // 2, 2, pieces // 2, 2)
    fine = Mesh(mesh.devices.reshape(sizes), ("z", "x", "y", "c"))
    blk, mp = ("z", "x"), ("y", "c")
    in_specs = (P(blk, None), P(None, None, mp), P(mp, None), P(blk, None), P(), P())
    out_specs = (P(blk, mp), P(None, blk, mp), P(mp, blk))
    return jax.shard_map(
        functools.partial(local, sizes), mesh=fine, in_specs=in_specs, out_specs=out_specs, check_vma=False
    )
```

```python
import functools
import math

import jax
import jax.numpy as jnp
from jax import lax
from jax.experimental import pallas as pl
from jax.experimental.pallas import tpu as pltpu
from jax.sharding import Mesh
from jax.sharding import PartitionSpec as P

HEAD = 128
BLOCK = 128
NEG_FILL = -1e30
BF16 = jnp.bfloat16
F32 = jnp.float32
MIB = 2**20

VMEM = pl.BlockSpec(memory_space=pltpu.VMEM)
SMEM = pl.BlockSpec(memory_space=pltpu.SMEM)
ANY = pl.BlockSpec(memory_space=pl.ANY)


def dot(a, b, dims):
    return lax.dot_general(a, b, (dims, ((), ())), preferred_element_type=F32)


def load_rows(parts, held, sems):
    copies, at = [], 0
    for i, part in enumerate(parts):
        rows = part.shape[-2]
        to = held.at[:, pl.ds(at, rows)] if len(part.shape) == 3 else held.at[pl.ds(at, rows)]
        copies.append(pltpu.make_async_copy(part, to, sems.at[i]))
        at += rows
    return copies


SPLIT = 4


def load_pieces(parts, piece, held, sems):
    copies, n = [], len(parts)
    for i, part in enumerate(parts):
        for j in range(part.shape[0] // piece):
            at = j * n + i
            copies.append(
                pltpu.make_async_copy(
                    part.at[pl.ds(j * piece, piece)], held.at[pl.ds(at * piece, piece)], sems.at[at]
                )
            )
    return copies


def load_weights(w_ref, w_held, sems):
    copies = []
    rows = w_ref.shape[1] // SPLIT
    for c in range(3):
        for i in range(SPLIT):
            at = pl.ds(i * rows, rows)
            copies.append(pltpu.make_async_copy(w_ref.at[c, at], w_held.at[c, at], sems.at[c * SPLIT + i]))
    return copies


def load_groups(groups, piece, held, sems):
    copies, at = [], 0
    for group in groups:
        size = piece if len(group) > 1 else group[0].shape[0]
        rows = sum(p.shape[0] for p in group)
        to = held.at[pl.ds(at, rows)]
        copies += load_pieces(group, size, to, sems.at[pl.ds(at // piece, rows // size)])
        at += rows
    return copies


def cut(parts, counts):
    groups, at = [], 0
    for n in counts:
        groups.append(parts[at : at + n])
        at += n
    return groups


def project_kernel(counts, piece, tok, *refs):
    n = sum(counts)
    parts, (w_ref, qkv_ref, held, sems) = refs[:n], refs[n:]

    @pl.when(pl.program_id(0) == 0)
    def _():
        copies = load_groups(cut(parts, counts), piece, held, sems)
        for copy in copies:
            copy.start()
        for copy in copies:
            copy.wait()

    for i in range(0, held.shape[0], tok):
        qkv_ref[0, i : i + tok] = dot(held[i : i + tok], w_ref[0], ((1,), (0,))).astype(BF16)


def project(groups, piece, w_qkv):
    counts = [len(g) for g in groups]
    parts = [p for g in groups for p in g]
    rows = sum(p.shape[0] for p in parts)
    tok = groups[0][0].shape[0]
    _, width, heads = w_qkv.shape
    n = len(parts)
    return pl.pallas_call(
        functools.partial(project_kernel, counts, piece, tok),
        grid=(3,),
        out_shape=jax.ShapeDtypeStruct((3, rows, heads), BF16),
        in_specs=[ANY] * n + [pl.BlockSpec((1, width, heads), lambda c: (c, 0, 0))],
        out_specs=pl.BlockSpec((1, rows, heads), lambda c: (c, 0, 0)),
        scratch_shapes=[pltpu.VMEM((rows, width), BF16), pltpu.SemaphoreType.DMA((rows // piece,))],
        compiler_params=pltpu.CompilerParams(vmem_limit_bytes=32 * MIB),
        cost_estimate=pl.CostEstimate(
            flops=6 * rows * width * heads, bytes_accessed=2 * (3 * heads * (width + rows) + rows * width), transcendentals=0
        ),
        name="project",
    )(*parts, w_qkv)


def cotangent_kernel(pieces, at_ref, grad_y_ref, w_ref, own_ref, sent_ref, cols_ref):
    quarter, chunk = at_ref[0], at_ref[1]
    chunks, tok, cols = cols_ref.shape
    piece = tok // pieces
    own_ref[...] = dot(grad_y_ref[...], w_ref[...], ((1,), (1,))).astype(BF16)
    for i in range(pieces):
        source = pl.ds(pl.multiple_of((quarter ^ i) * piece, piece), piece)
        to = slice(i * piece, (i + 1) * piece)
        sent_ref[to] = own_ref[source]
        for d in range(chunks):
            cols_ref[d, to] = grad_y_ref[source, d * cols : (d + 1) * cols]
    here = pl.ds(pl.multiple_of(chunk * cols, cols), cols)
    cols_ref[chunk] = grad_y_ref[:, here]


def cotangent(quarter, chunk, grad_y, w_out, pieces, chunks):
    tok, width = grad_y.shape
    heads = w_out.shape[0]
    return pl.pallas_call(
        functools.partial(cotangent_kernel, pieces),
        out_shape=(
            jax.ShapeDtypeStruct((tok, heads), BF16),
            jax.ShapeDtypeStruct((tok, heads), BF16),
            jax.ShapeDtypeStruct((chunks, tok, width // chunks), BF16),
        ),
        in_specs=[SMEM, VMEM, VMEM],
        out_specs=(VMEM, VMEM, VMEM),
        compiler_params=pltpu.CompilerParams(vmem_limit_bytes=60 * MIB),
        cost_estimate=pl.CostEstimate(
            flops=2 * tok * width * heads, bytes_accessed=2 * width * (2 * tok + heads), transcendentals=0
        ),
        name="cotangent",
    )(jnp.stack([quarter, chunk]), grad_y, w_out)


def attention_kernel(n_qkv, g_places, n_late, piece, tok, cols_ref, count_ref, home_ref, place_ref, *refs):
    refs, late = refs[n_late:], refs[:n_late]
    n_g = len(g_places)
    qkv_parts, g_parts = refs[:n_qkv], refs[n_qkv : n_qkv + n_g]
    (w_ref, grads_out, att_ref, sent_ref, kept_ref, qkv_ref, g_ref, dk_ref, dv_ref, grads_ref, w_held, held) = refs[n_qkv + n_g : -5]
    qkv_sems, g_sems, w_sems, out_sems, late_sems = refs[-5:]
    row_blocks, slots = cols_ref.shape
    heads = g_ref.shape[1] // HEAD
    scale = 1.0 / math.sqrt(HEAD)
    copies = load_rows(qkv_parts, qkv_ref, qkv_sems)
    for part, places in zip(g_parts, g_places):
        for i, at in enumerate(places):
            to = g_ref.at[pl.ds(at * tok, tok)]
            copies.append(pltpu.make_async_copy(part.at[pl.ds(i * tok, tok)], to, g_sems.at[at]))
    weights = load_weights(w_ref, w_held, w_sems)
    late_copies = load_pieces(late, piece, held, late_sems)
    for copy in late_copies + weights + copies:
        copy.start()
    dk_ref[...] = jnp.zeros_like(dk_ref)
    dv_ref[...] = jnp.zeros_like(dv_ref)
    for copy in late_copies:
        copy.wait()
    first = qkv_ref.shape[1] - held.shape[0]
    for c in range(3):
        for copy in weights[c * SPLIT : (c + 1) * SPLIT]:
            copy.wait()
        for i in range(0, held.shape[0], tok):
            qkv_ref[c, first + i : first + i + tok] = dot(held[i : i + tok], w_held[c], ((1,), (0,))).astype(BF16)
    for copy in copies:
        copy.wait()

    def row(r, carry):
        rows = pl.ds(pl.multiple_of(r * BLOCK, BLOCK), BLOCK)
        at = [pl.ds(pl.multiple_of(cols_ref[r, s] * BLOCK, BLOCK), BLOCK) for s in range(slots)]
        live = count_ref[r]
        home = pl.ds(pl.multiple_of(home_ref[r] * BLOCK, BLOCK), BLOCK)
        for h in range(heads):
            lanes = slice(h * HEAD, (h + 1) * HEAD)
            q = qkv_ref[0, rows, lanes]
            g = g_ref[rows, lanes]
            k = jnp.concatenate([qkv_ref[1, a, lanes] for a in at], axis=0)
            v = jnp.concatenate([qkv_ref[2, a, lanes] for a in at], axis=0)
            s = dot(k, q, ((1,), (1,))) * scale
            slot_of = lax.broadcasted_iota(jnp.int32, s.shape, 0) // BLOCK
            s = jnp.where(slot_of < live, s, NEG_FILL)
            e = jnp.exp(s - jnp.max(s, axis=0, keepdims=True))
            p = e * (1.0 / jnp.sum(e, axis=0, keepdims=True))
            p16 = p.astype(BF16)
            att_ref[home, lanes] = dot(p16, v, ((0,), (0,))).astype(BF16)
            dp = dot(v, g, ((1,), (1,)))
            delta = jnp.sum(p * dp, axis=0, keepdims=True)
            ds16 = (p * (dp - delta)).astype(BF16)
            grads_ref[0, rows, lanes] = (dot(ds16, k, ((0,), (0,))) * scale).astype(BF16)
            dk = dot(ds16, q, ((1,), (0,)))
            dv = dot(p16, g, ((1,), (0,)))
            for i, a in enumerate(at):
                part = slice(i * BLOCK, (i + 1) * BLOCK)
                dk_ref[a, lanes] += dk[part]
                dv_ref[a, lanes] += dv[part]
        return carry

    lax.fori_loop(0, row_blocks, row, 0)
    stores = [pltpu.make_async_copy(grads_ref.at[c], grads_out.at[c], out_sems.at[c]) for c in range(3)]
    stores[0].start()
    grads_ref[1] = (dk_ref[...] * scale).astype(BF16)
    stores[1].start()
    grads_ref[2] = dv_ref[...].astype(BF16)
    stores[2].start()

    def part(i):
        cols = kept_ref.shape[2]
        at = pl.ds(pl.multiple_of(place_ref[i] * cols, cols), cols)
        return sum(dot(grads_ref[c, :tok], w_held[c, at], ((1,), (1,))) for c in range(3))

    n_sent, n_kept = sent_ref.shape[0], kept_ref.shape[0]
    for i in range(n_sent):
        sent_ref[i] = part(i).astype(BF16)
    for i in range(n_kept):
        kept_ref[i] = part(n_sent + i)
    for copy in stores:
        copy.wait()


def attention(cols, count, home, places, n_kept, late, piece, qkv_parts, g_parts, g_places, w_qkv, tok, mp_cols):
    tokens = sum(p.shape[0] for p in g_parts)
    width = g_parts[0].shape[1]
    n_qkv, n_g = len(qkv_parts), len(g_parts)
    n_late, late_rows = len(late), sum(p.shape[0] for p in late)
    n_sent = places.shape[0] - n_kept
    return pl.pallas_call(
        functools.partial(attention_kernel, n_qkv, g_places, n_late, piece, tok),
        out_shape=(
            jax.ShapeDtypeStruct((3, tokens, width), BF16),
            jax.ShapeDtypeStruct((tokens, width), BF16),
            jax.ShapeDtypeStruct((n_sent, tok, mp_cols), BF16),
            jax.ShapeDtypeStruct((n_kept, tok, mp_cols), F32),
        ),
        in_specs=[SMEM] * 4 + [ANY] * (n_late + n_qkv + n_g + 1),
        out_specs=(ANY, VMEM, VMEM, VMEM),
        scratch_shapes=[
            pltpu.VMEM((3, tokens, width), BF16),
            pltpu.VMEM((tokens, width), BF16),
            pltpu.VMEM((tokens, width), F32),
            pltpu.VMEM((tokens, width), F32),
            pltpu.VMEM((3, tokens, width), BF16),
            pltpu.VMEM(w_qkv.shape, BF16),
            pltpu.VMEM((late_rows, late[0].shape[1]), BF16),
            pltpu.SemaphoreType.DMA((n_qkv,)),
            pltpu.SemaphoreType.DMA((tokens // tok,)),
            pltpu.SemaphoreType.DMA((3 * SPLIT,)),
            pltpu.SemaphoreType.DMA((3,)),
            pltpu.SemaphoreType.DMA((late_rows // piece,)),
        ],
        compiler_params=pltpu.CompilerParams(vmem_limit_bytes=60 * MIB),
        cost_estimate=pl.CostEstimate(flops=10**10, bytes_accessed=30 * MIB, transcendentals=0),
        name="attention",
    )(cols, count, home, places, *late, *qkv_parts, *g_parts, w_qkv)


def weight_grad_kernel(counts, piece, chunk_ref, *refs):
    n = sum(counts)
    parts, (grads_ref, out_ref, held, cols_held, sems, cols_sems) = refs[:n], refs[n:]
    rows = held.shape[1] // SPLIT
    cols = cols_held.shape[1]
    here = pl.ds(pl.multiple_of(chunk_ref[0] * cols, cols), cols)
    groups = cut([p.at[:, here] for p in parts], counts)
    loads = load_groups(groups, piece, cols_held, cols_sems)
    grad_loads = []
    for c in range(3):
        for i in range(SPLIT):
            at = pl.ds(i * rows, rows)
            grad_loads.append(pltpu.make_async_copy(grads_ref.at[c, at], held.at[c, at], sems.at[c * SPLIT + i]))
    for load in loads + grad_loads:
        load.start()
    for load in loads:
        load.wait()
    turned = cols_held[...].T
    for c in range(3):
        for load in grad_loads[c * SPLIT : (c + 1) * SPLIT]:
            load.wait()
        out_ref[c] = dot(turned, held[c], ((1,), (0,))).astype(BF16)


def weight_grad(chunk, groups, piece, grads, cols):
    counts = [len(g) for g in groups]
    token_parts = [p for g in groups for p in g]
    n = len(token_parts)
    _, tokens, heads = grads.shape
    return pl.pallas_call(
        functools.partial(weight_grad_kernel, counts, piece),
        in_specs=[SMEM] + [ANY] * (n + 1),
        out_specs=VMEM,
        out_shape=jax.ShapeDtypeStruct((3, cols, heads), BF16),
        scratch_shapes=[
            pltpu.VMEM(grads.shape, BF16),
            pltpu.VMEM((tokens, cols), BF16),
            pltpu.SemaphoreType.DMA((3 * SPLIT,)),
            pltpu.SemaphoreType.DMA((tokens // piece,)),
        ],
        compiler_params=pltpu.CompilerParams(vmem_limit_bytes=60 * MIB),
        cost_estimate=pl.CostEstimate(
            flops=6 * tokens * cols * heads, bytes_accessed=6 * tokens * heads, transcendentals=0
        ),
        name="weight_grad",
    )(chunk, *token_parts, grads)


def local(sizes, tokens_in, w_qkv, w_out, grad_y, block_cols, block_count):
    nz, nx, ny, nc = sizes
    mesh_size = dict(z=nz, x=nx, y=ny, c=nc)
    chunks, pieces = nz * nx, ny * nc
    tok, width = tokens_in.shape
    piece = tok // pieces
    out_cols = width // chunks
    blocks = tok // BLOCK
    y, c = lax.axis_index("y"), lax.axis_index("c")
    chunk = lax.axis_index("z") * nx + lax.axis_index("x")
    quarter = y * nc + c
    quarter_block = quarter * blocks // pieces

    def swap(a, axis, k):
        n = mesh_size[axis]
        return lax.ppermute(a, axis, [(i, i ^ k) for i in range(n)])

    def my_piece(a, k):
        return lax.dynamic_slice_in_dim(a, (quarter ^ k) * piece, piece, 0)

    def after(a, *done):
        return lax.optimization_barrier((a, done))[0]

    batches = [[1, 2], [4, 3], [i for k in range(3, nz) for i in (2 * k, 2 * k - 1)] + [2 * nz - 1]]
    order = [0] + [k for batch in batches for k in batch]
    g_own, g_sent, y_sent = cotangent(quarter, chunk, grad_y, w_out, pieces, chunks)

    def along_z(held, start, k):
        low = k & -k
        held[2 * k] = swap(start if k == low else held[2 * (k ^ low)], "z", low)

    own = my_piece(tokens_in, 0)
    got = {}
    for k in range(1, nz):
        along_z(got, own, k)
    got[1] = swap(own, "x", 1)
    got[3] = swap(after(got[2], got[1], g_own), "x", 1)
    last_x = got[3]
    for k in range(2, nz - 1):
        got[2 * k + 1] = last_x = swap(after(got[2 * k], last_x), "x", 1)
    got[2 * nz - 1] = swap(got[2 * nz - 3], "z", 1)

    groups = [[tokens_in]]
    behind, qkv_parts = [], []
    for at, batch in enumerate(batches):
        mine = jnp.concatenate([got[k] for k in batch], axis=0)
        ys = [mine] + [swap(after(mine, *behind), "y", i) for i in range(1, ny)]
        behind = ys[1:]
        parts = []
        for i, a in enumerate(ys):
            core = after(a, *qkv_parts) if i == 0 else a
            parts += [a] + [swap(core, "c", j) for j in range(1, nc)]
        groups.append(parts)
        if at == 1:
            qkv_parts = [project(groups, piece, w_qkv)]
    late = groups[-1]

    g = {0: g_own, 1: swap(after(g_sent, last_x), "x", 1)}
    g_late = after(g_sent, got[2 * nz - 1])
    for k in range(1, nz):
        along_z(g, g_late, k)
    g_far = [g[2 * k] for k in range(1, nz)]
    g_x = swap(after(jnp.concatenate(g_far, axis=0), g[1]), "x", 1)
    g_parts = [g_own, g[1]] + g_far + [g_x]
    g_places, at = [], 0
    g_order = [0, 1] + [2 * k for k in range(1, nz)] + [2 * k + 1 for k in range(1, nz)]
    for part in g_parts:
        n = part.shape[0] // tok
        g_places.append([order.index(k) for k in g_order[at : at + n]])
        at += n

    y_sent = after(y_sent, *g_far)
    y_all = lax.all_to_all(y_sent, ("z", "x"), 0, 0, tiled=True).reshape(chunks * tok, out_cols)

    held = jnp.repeat(jnp.array(order, jnp.int32), blocks)
    inner = jnp.tile(jnp.arange(blocks, dtype=jnp.int32), chunks)
    number = jnp.arange(chunks * blocks, dtype=jnp.int32)

    def flip(k):
        return jnp.where(k == 0, 0, quarter_block)

    block_at = (held ^ chunk) * blocks + (inner ^ flip(held))
    pick = block_at[:, None] == number[None, :]
    cols = jnp.sum(jnp.where(pick[:, :, None], block_cols[None], 0), axis=1)
    count = jnp.sum(jnp.where(pick, block_count[None], 0), axis=1)
    cols = jnp.sum(jnp.where(cols[:, :, None] == block_at[None, None, :], number[None, None, :], 0), axis=2)
    home = (held ^ chunk) * blocks + inner

    by_y = y ^ jnp.arange(ny, dtype=jnp.int32)
    places = jnp.concatenate([by_y * nc + (c ^ j) for j in range(1, nc)] + [by_y * nc + c])
    grads, att, sent, half = attention(
        cols, count, home, places, ny, late, piece, qkv_parts, g_parts, g_places, w_qkv, tok, width // pieces
    )
    for j in range(1, nc):
        half = half + swap(sent[(j - 1) * ny : j * ny], "c", j).astype(F32)
    grad_x = half[0]
    for k in range(1, ny):
        grad_x = grad_x + swap(half[k].astype(BF16), "y", k).astype(F32)

    grad_qkv = weight_grad(chunk.reshape(1), groups, piece, grads, out_cols)
    grad_out = dot(att, y_all, ((0,), (0,))).astype(BF16)
    return (grad_x.astype(BF16), grad_qkv, grad_out)


def solution(mesh):
    chunks, pieces = mesh.shape["blk"], mesh.shape["mp"]
    sizes = (chunks // 2, 2, pieces // 2, 2)
    fine = Mesh(mesh.devices.reshape(sizes), ("z", "x", "y", "c"))
    blk, mp = ("z", "x"), ("y", "c")
    in_specs = (P(blk, None), P(None, None, mp), P(mp, None), P(blk, None), P(), P())
    out_specs = (P(blk, mp), P(None, blk, mp), P(mp, blk))
    return jax.shard_map(
        functools.partial(local, sizes), mesh=fine, in_specs=in_specs, out_specs=out_specs, check_vma=False
    )
```

```python
import functools
import math

import jax
import jax.numpy as jnp
from jax import lax
from jax.experimental import pallas as pl
from jax.experimental.pallas import tpu as pltpu
from jax.sharding import Mesh
from jax.sharding import PartitionSpec as P

HEAD = 128
BLOCK = 128
NEG_FILL = -1e30
BF16 = jnp.bfloat16
F32 = jnp.float32
MIB = 2**20

VMEM = pl.BlockSpec(memory_space=pltpu.VMEM)
SMEM = pl.BlockSpec(memory_space=pltpu.SMEM)
ANY = pl.BlockSpec(memory_space=pl.ANY)


def dot(a, b, dims):
    return lax.dot_general(a, b, (dims, ((), ())), preferred_element_type=F32)


def load_rows(parts, held, sems):
    copies, at = [], 0
    for i, part in enumerate(parts):
        rows = part.shape[-2]
        to = held.at[:, pl.ds(at, rows)] if len(part.shape) == 3 else held.at[pl.ds(at, rows)]
        copies.append(pltpu.make_async_copy(part, to, sems.at[i]))
        at += rows
    return copies


SPLIT = 4
ROWS = 2


def load_pieces(parts, piece, held, sems):
    copies, n = [], len(parts)
    for i, part in enumerate(parts):
        for j in range(part.shape[0] // piece):
            at = j * n + i
            copies.append(
                pltpu.make_async_copy(
                    part.at[pl.ds(j * piece, piece)], held.at[pl.ds(at * piece, piece)], sems.at[at]
                )
            )
    return copies


def load_weights(w_ref, w_held, sems):
    copies = []
    rows = w_ref.shape[1] // SPLIT
    for c in range(3):
        for i in range(SPLIT):
            at = pl.ds(i * rows, rows)
            copies.append(pltpu.make_async_copy(w_ref.at[c, at], w_held.at[c, at], sems.at[c * SPLIT + i]))
    return copies


def load_groups(groups, piece, held, sems):
    copies, at = [], 0
    for group in groups:
        size = piece if len(group) > 1 else group[0].shape[0]
        rows = sum(p.shape[0] for p in group)
        to = held.at[pl.ds(at, rows)]
        copies += load_pieces(group, size, to, sems.at[pl.ds(at // piece, rows // size)])
        at += rows
    return copies


def join_kernel(*refs):
    at = 0
    for part in refs[:-1]:
        refs[-1][at : at + part.shape[0]] = part[...]
        at += part.shape[0]


def join(parts):
    rows = sum(p.shape[0] for p in parts)
    cols = parts[0].shape[1]
    return pl.pallas_call(
        join_kernel,
        out_shape=jax.ShapeDtypeStruct((rows, cols), parts[0].dtype),
        in_specs=[VMEM] * len(parts),
        out_specs=VMEM,
        cost_estimate=pl.CostEstimate(flops=0, bytes_accessed=4 * rows * cols, transcendentals=0),
        name="join",
    )(*parts)


def cut(parts, counts):
    groups, at = [], 0
    for n in counts:
        groups.append(parts[at : at + n])
        at += n
    return groups


def project_kernel(counts, piece, tok, *refs):
    n = sum(counts)
    parts, (w_ref, qkv_ref, held, sems) = refs[:n], refs[n:]

    @pl.when(pl.program_id(0) == 0)
    def _():
        copies = load_groups(cut(parts, counts), piece, held, sems)
        for copy in copies:
            copy.start()
        for copy in copies:
            copy.wait()

    for i in range(0, held.shape[0], tok):
        qkv_ref[0, i : i + tok] = dot(held[i : i + tok], w_ref[0], ((1,), (0,))).astype(BF16)


def project(groups, piece, w_qkv):
    counts = [len(g) for g in groups]
    parts = [p for g in groups for p in g]
    rows = sum(p.shape[0] for p in parts)
    tok = groups[0][0].shape[0]
    _, width, heads = w_qkv.shape
    n = len(parts)
    return pl.pallas_call(
        functools.partial(project_kernel, counts, piece, tok),
        grid=(3,),
        out_shape=jax.ShapeDtypeStruct((3, rows, heads), BF16),
        in_specs=[ANY] * n + [pl.BlockSpec((1, width, heads), lambda c: (c, 0, 0))],
        out_specs=pl.BlockSpec((1, rows, heads), lambda c: (c, 0, 0)),
        scratch_shapes=[pltpu.VMEM((rows, width), BF16), pltpu.SemaphoreType.DMA((rows // piece,))],
        compiler_params=pltpu.CompilerParams(vmem_limit_bytes=32 * MIB),
        cost_estimate=pl.CostEstimate(
            flops=6 * rows * width * heads, bytes_accessed=2 * (3 * heads * (width + rows) + rows * width), transcendentals=0
        ),
        name="project",
    )(*parts, w_qkv)


def cotangent_kernel(pieces, at_ref, grad_y_ref, w_ref, own_ref, sent_ref, cols_ref):
    quarter, chunk = at_ref[0], at_ref[1]
    chunks, tok, cols = cols_ref.shape
    piece = tok // pieces
    own_ref[...] = dot(grad_y_ref[...], w_ref[...], ((1,), (1,))).astype(BF16)
    for i in range(pieces):
        source = pl.ds(pl.multiple_of((quarter ^ i) * piece, piece), piece)
        to = slice(i * piece, (i + 1) * piece)
        sent_ref[to] = own_ref[source]
        for d in range(chunks):
            cols_ref[d, to] = grad_y_ref[source, d * cols : (d + 1) * cols]
    here = pl.ds(pl.multiple_of(chunk * cols, cols), cols)
    cols_ref[chunk] = grad_y_ref[:, here]


def cotangent(quarter, chunk, grad_y, w_out, pieces, chunks):
    tok, width = grad_y.shape
    heads = w_out.shape[0]
    return pl.pallas_call(
        functools.partial(cotangent_kernel, pieces),
        out_shape=(
            jax.ShapeDtypeStruct((tok, heads), BF16),
            jax.ShapeDtypeStruct((tok, heads), BF16),
            jax.ShapeDtypeStruct((chunks, tok, width // chunks), BF16),
        ),
        in_specs=[SMEM, VMEM, VMEM],
        out_specs=(VMEM, VMEM, VMEM),
        compiler_params=pltpu.CompilerParams(vmem_limit_bytes=60 * MIB),
        cost_estimate=pl.CostEstimate(
            flops=2 * tok * width * heads, bytes_accessed=2 * width * (2 * tok + heads), transcendentals=0
        ),
        name="cotangent",
    )(jnp.stack([quarter, chunk]), grad_y, w_out)


def attention_kernel(n_qkv, g_places, late_counts, piece, tok, cols_ref, count_ref, home_ref, place_ref, *refs):
    n_late = sum(late_counts)
    refs, late = refs[n_late:], refs[:n_late]
    n_g = len(g_places)
    qkv_parts, g_parts = refs[:n_qkv], refs[n_qkv : n_qkv + n_g]
    (w_ref, grads_out, att_ref, sent_ref, kept_ref, qkv_ref, g_ref, dk_ref, dv_ref, grads_ref, w_held, held) = refs[n_qkv + n_g : -5]
    qkv_sems, g_sems, w_sems, out_sems, late_sems = refs[-5:]
    row_blocks, slots = cols_ref.shape
    heads = g_ref.shape[1] // HEAD
    scale = 1.0 / math.sqrt(HEAD)
    copies = load_rows(qkv_parts, qkv_ref, qkv_sems)
    for part, places in zip(g_parts, g_places):
        for i, at in enumerate(places):
            to = g_ref.at[pl.ds(at * tok, tok)]
            copies.append(pltpu.make_async_copy(part.at[pl.ds(i * tok, tok)], to, g_sems.at[at]))
    weights = load_weights(w_ref, w_held, w_sems)
    late_copies = load_groups(cut(late, late_counts), piece, held, late_sems)
    for copy in late_copies + weights + copies:
        copy.start()
    dk_ref[...] = jnp.zeros_like(dk_ref)
    dv_ref[...] = jnp.zeros_like(dv_ref)
    for copy in late_copies:
        copy.wait()
    first = qkv_ref.shape[1] - held.shape[0]
    for c in range(3):
        for copy in weights[c * SPLIT : (c + 1) * SPLIT]:
            copy.wait()
        for i in range(0, held.shape[0], tok):
            qkv_ref[c, first + i : first + i + tok] = dot(held[i : i + tok], w_held[c], ((1,), (0,))).astype(BF16)
    for copy in copies:
        copy.wait()

    def some_rows(step, carry):
        units = []
        for i in range(ROWS):
            r = step * ROWS + i
            rows = pl.ds(pl.multiple_of(r * BLOCK, BLOCK), BLOCK)
            at = [pl.ds(pl.multiple_of(cols_ref[r, s] * BLOCK, BLOCK), BLOCK) for s in range(slots)]
            home = pl.ds(pl.multiple_of(home_ref[r] * BLOCK, BLOCK), BLOCK)
            for h in range(heads):
                units.append((rows, at, home, count_ref[r], slice(h * HEAD, (h + 1) * HEAD)))
        q = [qkv_ref[0, rows, lane] for rows, _, _, _, lane in units]
        g = [g_ref[rows, lane] for rows, _, _, _, lane in units]
        k = [jnp.concatenate([qkv_ref[1, a, lane] for a in at], axis=0) for _, at, _, _, lane in units]
        v = [jnp.concatenate([qkv_ref[2, a, lane] for a in at], axis=0) for _, at, _, _, lane in units]
        s = [dot(a, b, ((1,), (1,))) * scale for a, b in zip(k, q)]
        dp = [dot(a, b, ((1,), (1,))) for a, b in zip(v, g)]
        slot_of = lax.broadcasted_iota(jnp.int32, s[0].shape, 0) // BLOCK
        p, p16, ds16 = [], [], []
        for u, unit in enumerate(units):
            kept = jnp.where(slot_of < unit[3], s[u], NEG_FILL)
            e = jnp.exp(kept - jnp.max(kept, axis=0, keepdims=True))
            p.append(e * (1.0 / jnp.sum(e, axis=0, keepdims=True)))
            p16.append(p[u].astype(BF16))
        for u in range(len(units)):
            delta = jnp.sum(p[u] * dp[u], axis=0, keepdims=True)
            ds16.append((p[u] * (dp[u] - delta)).astype(BF16))
        for u, (rows, _, home, _, lane) in enumerate(units):
            att_ref[home, lane] = dot(p16[u], v[u], ((0,), (0,))).astype(BF16)
            grads_ref[0, rows, lane] = (dot(ds16[u], k[u], ((0,), (0,))) * scale).astype(BF16)
        for u, (_, at, _, _, lane) in enumerate(units):
            dk = dot(ds16[u], q[u], ((1,), (0,)))
            dv = dot(p16[u], g[u], ((1,), (0,)))
            for i, a in enumerate(at):
                part = slice(i * BLOCK, (i + 1) * BLOCK)
                dk_ref[a, lane] += dk[part]
                dv_ref[a, lane] += dv[part]
        return carry

    lax.fori_loop(0, row_blocks // ROWS, some_rows, 0)
    stores = [pltpu.make_async_copy(grads_ref.at[c], grads_out.at[c], out_sems.at[c]) for c in range(3)]
    stores[0].start()
    grads_ref[1] = (dk_ref[...] * scale).astype(BF16)
    stores[1].start()
    grads_ref[2] = dv_ref[...].astype(BF16)
    stores[2].start()

    def part(i):
        cols = kept_ref.shape[2]
        at = pl.ds(pl.multiple_of(place_ref[i] * cols, cols), cols)
        return sum(dot(grads_ref[c, :tok], w_held[c, at], ((1,), (1,))) for c in range(3))

    n_sent, n_kept = sent_ref.shape[0], kept_ref.shape[0]
    for i in range(n_sent):
        sent_ref[i] = part(i).astype(BF16)
    for i in range(n_kept):
        kept_ref[i] = part(n_sent + i)
    for copy in stores:
        copy.wait()


def attention(cols, count, home, places, n_kept, late, piece, qkv_parts, g_parts, g_places, w_qkv, tok, mp_cols):
    tokens = sum(p.shape[0] for p in g_parts)
    width = g_parts[0].shape[1]
    n_qkv, n_g = len(qkv_parts), len(g_parts)
    late_counts = [len(group) for group in late]
    late = [p for group in late for p in group]
    n_late, late_rows = len(late), sum(p.shape[0] for p in late)
    n_sent = places.shape[0] - n_kept
    return pl.pallas_call(
        functools.partial(attention_kernel, n_qkv, g_places, late_counts, piece, tok),
        out_shape=(
            jax.ShapeDtypeStruct((3, tokens, width), BF16),
            jax.ShapeDtypeStruct((tokens, width), BF16),
            jax.ShapeDtypeStruct((n_sent, tok, mp_cols), BF16),
            jax.ShapeDtypeStruct((n_kept, tok, mp_cols), F32),
        ),
        in_specs=[SMEM] * 4 + [ANY] * (n_late + n_qkv + n_g + 1),
        out_specs=(ANY, VMEM, VMEM, VMEM),
        scratch_shapes=[
            pltpu.VMEM((3, tokens, width), BF16),
            pltpu.VMEM((tokens, width), BF16),
            pltpu.VMEM((tokens, width), F32),
            pltpu.VMEM((tokens, width), F32),
            pltpu.VMEM((3, tokens, width), BF16),
            pltpu.VMEM(w_qkv.shape, BF16),
            pltpu.VMEM((late_rows, late[0].shape[1]), BF16),
            pltpu.SemaphoreType.DMA((n_qkv,)),
            pltpu.SemaphoreType.DMA((tokens // tok,)),
            pltpu.SemaphoreType.DMA((3 * SPLIT,)),
            pltpu.SemaphoreType.DMA((3,)),
            pltpu.SemaphoreType.DMA((late_rows // piece,)),
        ],
        compiler_params=pltpu.CompilerParams(vmem_limit_bytes=60 * MIB),
        cost_estimate=pl.CostEstimate(flops=10**10, bytes_accessed=30 * MIB, transcendentals=0),
        name="attention",
    )(cols, count, home, places, *late, *qkv_parts, *g_parts, w_qkv)


def weight_grad_kernel(counts, piece, chunk_ref, *refs):
    n = sum(counts)
    parts, (grads_ref, out_ref, held, cols_held, sems, cols_sems) = refs[:n], refs[n:]
    rows = held.shape[1] // SPLIT
    cols = cols_held.shape[1]
    here = pl.ds(pl.multiple_of(chunk_ref[0] * cols, cols), cols)
    groups = cut([p.at[:, here] for p in parts], counts)
    loads = load_groups(groups, piece, cols_held, cols_sems)
    grad_loads = []
    for c in range(3):
        for i in range(SPLIT):
            at = pl.ds(i * rows, rows)
            grad_loads.append(pltpu.make_async_copy(grads_ref.at[c, at], held.at[c, at], sems.at[c * SPLIT + i]))
    for load in loads + grad_loads:
        load.start()
    for load in loads:
        load.wait()
    turned = cols_held[...].T
    for c in range(3):
        for load in grad_loads[c * SPLIT : (c + 1) * SPLIT]:
            load.wait()
        out_ref[c] = dot(turned, held[c], ((1,), (0,))).astype(BF16)


def weight_grad(chunk, groups, piece, grads, cols):
    counts = [len(g) for g in groups]
    token_parts = [p for g in groups for p in g]
    n = len(token_parts)
    _, tokens, heads = grads.shape
    return pl.pallas_call(
        functools.partial(weight_grad_kernel, counts, piece),
        in_specs=[SMEM] + [ANY] * (n + 1),
        out_specs=VMEM,
        out_shape=jax.ShapeDtypeStruct((3, cols, heads), BF16),
        scratch_shapes=[
            pltpu.VMEM(grads.shape, BF16),
            pltpu.VMEM((tokens, cols), BF16),
            pltpu.SemaphoreType.DMA((3 * SPLIT,)),
            pltpu.SemaphoreType.DMA((tokens // piece,)),
        ],
        compiler_params=pltpu.CompilerParams(vmem_limit_bytes=60 * MIB),
        cost_estimate=pl.CostEstimate(
            flops=6 * tokens * cols * heads, bytes_accessed=6 * tokens * heads, transcendentals=0
        ),
        name="weight_grad",
    )(chunk, *token_parts, grads)


def local(sizes, tokens_in, w_qkv, w_out, grad_y, block_cols, block_count):
    nz, nx, ny, nc = sizes
    mesh_size = dict(z=nz, x=nx, y=ny, c=nc)
    chunks, pieces = nz * nx, ny * nc
    tok, width = tokens_in.shape
    piece = tok // pieces
    out_cols = width // chunks
    blocks = tok // BLOCK
    y, c = lax.axis_index("y"), lax.axis_index("c")
    chunk = lax.axis_index("z") * nx + lax.axis_index("x")
    quarter = y * nc + c
    quarter_block = quarter * blocks // pieces

    def swap(a, axis, k):
        n = mesh_size[axis]
        return lax.ppermute(a, axis, [(i, i ^ k) for i in range(n)])

    def my_piece(a, k):
        return lax.dynamic_slice_in_dim(a, (quarter ^ k) * piece, piece, 0)

    def after(a, *done):
        return lax.optimization_barrier((a, done))[0]

    batches = [[1, 2], [4, 3], [i for k in range(3, nz) for i in (2 * k, 2 * k - 1)] + [2 * nz - 1]]
    order = [0] + [k for batch in batches for k in batch]
    g_own, g_sent, y_sent = cotangent(quarter, chunk, grad_y, w_out, pieces, chunks)

    def along_z(held, start, k):
        low = k & -k
        held[2 * k] = swap(start if k == low else held[2 * (k ^ low)], "z", low)

    own = my_piece(tokens_in, 0)
    got = {}
    for k in range(1, nz):
        along_z(got, own, k)
    got[1] = swap(own, "x", 1)
    got[3] = swap(after(got[2], got[1], g_own), "x", 1)
    last_x = got[3]
    for k in range(2, nz):
        got[2 * k + 1] = last_x = swap(after(got[2 * k], last_x), "x", 1)

    g_x = swap(after(g_sent, last_x), "x", 1)
    g_z = {}
    for k in range(1, nz):
        low = k & -k
        g_z[k] = swap(after(g_sent, got[4]) if k == low else g_z[k ^ low], "z", low)
    g_far = [g_z[k] for k in range(1, nz)]
    g_far.append(swap(after(join(g_far), g_x), "x", 1))
    g_parts = [g_own, g_x] + g_far
    places = [[0], [1]] + [[2 * k] for k in range(1, nz)] + [[2 * k + 1 for k in range(1, nz)]]
    g_places = [[order.index(k) for k in part] for part in places]

    groups, behind, qkv_parts = [[tokens_in]], [], []
    for at, batch in enumerate(batches):
        first = after(got[batch[0]], *qkv_parts) if at == 2 else got[batch[0]]
        mine = join([first] + [got[k] for k in batch[1:]])
        ys = [mine] + [swap(after(mine, *behind), "y", i) for i in range(1, ny)]
        behind = ys[1:]
        parts = []
        for i, a in enumerate(ys):
            core = after(a, *ys[1:]) if i == 0 else a
            parts += [a] + [swap(core, "c", j) for j in range(1, nc)]
        groups.append(parts)
        if at == 0:
            qkv_parts = [project(groups, piece, w_qkv)]
    late = groups[2:]

    y_sent = after(y_sent, *g_far)
    y_all = lax.all_to_all(y_sent, ("z", "x"), 0, 0, tiled=True).reshape(chunks * tok, out_cols)

    held = jnp.repeat(jnp.array(order, jnp.int32), blocks)
    inner = jnp.tile(jnp.arange(blocks, dtype=jnp.int32), chunks)
    number = jnp.arange(chunks * blocks, dtype=jnp.int32)

    def flip(k):
        return jnp.where(k == 0, 0, quarter_block)

    block_at = (held ^ chunk) * blocks + (inner ^ flip(held))
    pick = block_at[:, None] == number[None, :]
    cols = jnp.sum(jnp.where(pick[:, :, None], block_cols[None], 0), axis=1)
    count = jnp.sum(jnp.where(pick, block_count[None], 0), axis=1)
    cols = jnp.sum(jnp.where(cols[:, :, None] == block_at[None, None, :], number[None, None, :], 0), axis=2)
    home = (held ^ chunk) * blocks + inner

    by_y = y ^ jnp.arange(ny, dtype=jnp.int32)
    places = jnp.concatenate([by_y * nc + (c ^ j) for j in range(1, nc)] + [by_y * nc + c])
    grads, att, sent, half = attention(
        cols, count, home, places, ny, late, piece, qkv_parts, g_parts, g_places, w_qkv, tok, width // pieces
    )
    grad_out = dot(att, y_all, ((0,), (0,))).astype(BF16)
    half = after(half, grad_out)
    for j in range(1, nc):
        half = half + swap(sent[(j - 1) * ny : j * ny], "c", j).astype(F32)
    grad_x = half[0]
    for k in range(1, ny):
        grad_x = grad_x + swap(half[k].astype(BF16), "y", k).astype(F32)

    grad_qkv = weight_grad(chunk.reshape(1), groups, piece, after(grads, half), out_cols)
    return (grad_x.astype(BF16), grad_qkv, grad_out)


def solution(mesh):
    chunks, pieces = mesh.shape["blk"], mesh.shape["mp"]
    sizes = (chunks // 2, 2, pieces // 2, 2)
    fine = Mesh(mesh.devices.reshape(sizes), ("z", "x", "y", "c"))
    blk, mp = ("z", "x"), ("y", "c")
    in_specs = (P(blk, None), P(None, None, mp), P(mp, None), P(blk, None), P(), P())
    out_specs = (P(blk, mp), P(None, blk, mp), P(mp, blk))
    return jax.shard_map(
        functools.partial(local, sizes), mesh=fine, in_specs=in_specs, out_specs=out_specs, check_vma=False
    )
```

```python
import functools
import math

import jax
import jax.numpy as jnp
from jax import lax
from jax.experimental import pallas as pl
from jax.experimental.pallas import tpu as pltpu
from jax.sharding import Mesh
from jax.sharding import PartitionSpec as P

HEAD = 128
BLOCK = 128
NEG_FILL = -1e30
BF16 = jnp.bfloat16
F32 = jnp.float32
MIB = 2**20

VMEM = pl.BlockSpec(memory_space=pltpu.VMEM)
SMEM = pl.BlockSpec(memory_space=pltpu.SMEM)
ANY = pl.BlockSpec(memory_space=pl.ANY)


def dot(a, b, dims):
    return lax.dot_general(a, b, (dims, ((), ())), preferred_element_type=F32)


def load_rows(parts, held, sems):
    copies, at = [], 0
    for i, part in enumerate(parts):
        rows = part.shape[-2]
        to = held.at[:, pl.ds(at, rows)] if len(part.shape) == 3 else held.at[pl.ds(at, rows)]
        copies.append(pltpu.make_async_copy(part, to, sems.at[i]))
        at += rows
    return copies


SPLIT = 4
ROWS = 2


def load_pieces(parts, piece, held, sems):
    copies, n = [], len(parts)
    for i, part in enumerate(parts):
        for j in range(part.shape[0] // piece):
            at = j * n + i
            copies.append(
                pltpu.make_async_copy(
                    part.at[pl.ds(j * piece, piece)], held.at[pl.ds(at * piece, piece)], sems.at[at]
                )
            )
    return copies


def load_weights(w_ref, w_held, sems):
    copies = []
    rows = w_ref.shape[1] // SPLIT
    for c in range(3):
        for i in range(SPLIT):
            at = pl.ds(i * rows, rows)
            copies.append(pltpu.make_async_copy(w_ref.at[c, at], w_held.at[c, at], sems.at[c * SPLIT + i]))
    return copies


def load_groups(groups, piece, held, sems):
    copies, at = [], 0
    for group in groups:
        size = piece if len(group) > 1 else group[0].shape[0]
        rows = sum(p.shape[0] for p in group)
        to = held.at[pl.ds(at, rows)]
        copies += load_pieces(group, size, to, sems.at[pl.ds(at // piece, rows // size)])
        at += rows
    return copies


def join_kernel(*refs):
    at = 0
    for part in refs[:-1]:
        refs[-1][at : at + part.shape[0]] = part[...]
        at += part.shape[0]


def join(parts):
    rows = sum(p.shape[0] for p in parts)
    cols = parts[0].shape[1]
    return pl.pallas_call(
        join_kernel,
        out_shape=jax.ShapeDtypeStruct((rows, cols), parts[0].dtype),
        in_specs=[VMEM] * len(parts),
        out_specs=VMEM,
        cost_estimate=pl.CostEstimate(flops=0, bytes_accessed=4 * rows * cols, transcendentals=0),
        name="join",
    )(*parts)


def cut(parts, counts):
    groups, at = [], 0
    for n in counts:
        groups.append(parts[at : at + n])
        at += n
    return groups


def project_kernel(counts, piece, tok, *refs):
    n = sum(counts)
    parts, (w_ref, qkv_ref, held, sems) = refs[:n], refs[n:]

    @pl.when(pl.program_id(0) == 0)
    def _():
        copies = load_groups(cut(parts, counts), piece, held, sems)
        for copy in copies:
            copy.start()
        for copy in copies:
            copy.wait()

    for i in range(0, held.shape[0], tok):
        qkv_ref[0, i : i + tok] = dot(held[i : i + tok], w_ref[0], ((1,), (0,))).astype(BF16)


def project(groups, piece, w_qkv):
    counts = [len(g) for g in groups]
    parts = [p for g in groups for p in g]
    rows = sum(p.shape[0] for p in parts)
    tok = groups[0][0].shape[0]
    _, width, heads = w_qkv.shape
    n = len(parts)
    return pl.pallas_call(
        functools.partial(project_kernel, counts, piece, tok),
        grid=(3,),
        out_shape=jax.ShapeDtypeStruct((3, rows, heads), BF16),
        in_specs=[ANY] * n + [pl.BlockSpec((1, width, heads), lambda c: (c, 0, 0))],
        out_specs=pl.BlockSpec((1, rows, heads), lambda c: (c, 0, 0)),
        scratch_shapes=[pltpu.VMEM((rows, width), BF16), pltpu.SemaphoreType.DMA((rows // piece,))],
        compiler_params=pltpu.CompilerParams(vmem_limit_bytes=32 * MIB),
        cost_estimate=pl.CostEstimate(
            flops=6 * rows * width * heads, bytes_accessed=2 * (3 * heads * (width + rows) + rows * width), transcendentals=0
        ),
        name="project",
    )(*parts, w_qkv)


def cotangent_kernel(pieces, at_ref, grad_y_ref, w_ref, own_ref, sent_ref, cols_ref):
    quarter, chunk = at_ref[0], at_ref[1]
    chunks, tok, cols = cols_ref.shape
    piece = tok // pieces
    own_ref[...] = dot(grad_y_ref[...], w_ref[...], ((1,), (1,))).astype(BF16)
    for i in range(pieces):
        source = pl.ds(pl.multiple_of((quarter ^ i) * piece, piece), piece)
        to = slice(i * piece, (i + 1) * piece)
        sent_ref[to] = own_ref[source]
        for d in range(chunks):
            cols_ref[d, to] = grad_y_ref[source, d * cols : (d + 1) * cols]
    here = pl.ds(pl.multiple_of(chunk * cols, cols), cols)
    cols_ref[chunk] = grad_y_ref[:, here]


def cotangent(quarter, chunk, grad_y, w_out, pieces, chunks):
    tok, width = grad_y.shape
    heads = w_out.shape[0]
    return pl.pallas_call(
        functools.partial(cotangent_kernel, pieces),
        out_shape=(
            jax.ShapeDtypeStruct((tok, heads), BF16),
            jax.ShapeDtypeStruct((tok, heads), BF16),
            jax.ShapeDtypeStruct((chunks, tok, width // chunks), BF16),
        ),
        in_specs=[SMEM, VMEM, VMEM],
        out_specs=(VMEM, VMEM, VMEM),
        compiler_params=pltpu.CompilerParams(vmem_limit_bytes=60 * MIB),
        cost_estimate=pl.CostEstimate(
            flops=2 * tok * width * heads, bytes_accessed=2 * width * (2 * tok + heads), transcendentals=0
        ),
        name="cotangent",
    )(jnp.stack([quarter, chunk]), grad_y, w_out)


def attention_kernel(n_qkv, g_places, late_counts, piece, tok, cols_ref, count_ref, home_ref, place_ref, *refs):
    n_late = sum(late_counts)
    refs, late = refs[n_late:], refs[:n_late]
    n_g = len(g_places)
    qkv_parts, g_parts = refs[:n_qkv], refs[n_qkv : n_qkv + n_g]
    (w_ref, grads_out, att_ref, sent_ref, kept_ref, qkv_ref, g_ref, dk_ref, dv_ref, grads_ref, w_held, held) = refs[n_qkv + n_g : -5]
    qkv_sems, g_sems, w_sems, out_sems, late_sems = refs[-5:]
    row_blocks, slots = cols_ref.shape
    heads = g_ref.shape[1] // HEAD
    scale = 1.0 / math.sqrt(HEAD)
    copies = load_rows(qkv_parts, qkv_ref, qkv_sems)
    for part, places in zip(g_parts, g_places):
        for i, at in enumerate(places):
            to = g_ref.at[pl.ds(at * tok, tok)]
            copies.append(pltpu.make_async_copy(part.at[pl.ds(i * tok, tok)], to, g_sems.at[at]))
    weights = load_weights(w_ref, w_held, w_sems)
    late_copies = load_groups(cut(late, late_counts), piece, held, late_sems)
    for copy in late_copies + weights + copies:
        copy.start()
    dk_ref[...] = jnp.zeros_like(dk_ref)
    dv_ref[...] = jnp.zeros_like(dv_ref)
    for copy in late_copies:
        copy.wait()
    first = qkv_ref.shape[1] - held.shape[0]
    for c in range(3):
        for copy in weights[c * SPLIT : (c + 1) * SPLIT]:
            copy.wait()
        for i in range(0, held.shape[0], tok):
            qkv_ref[c, first + i : first + i + tok] = dot(held[i : i + tok], w_held[c], ((1,), (0,))).astype(BF16)
    for copy in copies:
        copy.wait()

    def some_rows(step, carry):
        units = []
        for i in range(ROWS):
            r = step * ROWS + i
            rows = pl.ds(pl.multiple_of(r * BLOCK, BLOCK), BLOCK)
            at = [pl.ds(pl.multiple_of(cols_ref[r, s] * BLOCK, BLOCK), BLOCK) for s in range(slots)]
            home = pl.ds(pl.multiple_of(home_ref[r] * BLOCK, BLOCK), BLOCK)
            for h in range(heads):
                units.append((rows, at, home, count_ref[r], slice(h * HEAD, (h + 1) * HEAD)))
        q = [qkv_ref[0, rows, lane] for rows, _, _, _, lane in units]
        g = [g_ref[rows, lane] for rows, _, _, _, lane in units]
        k = [jnp.concatenate([qkv_ref[1, a, lane] for a in at], axis=0) for _, at, _, _, lane in units]
        v = [jnp.concatenate([qkv_ref[2, a, lane] for a in at], axis=0) for _, at, _, _, lane in units]
        s = [dot(a, b, ((1,), (1,))) * scale for a, b in zip(k, q)]
        dp = [dot(a, b, ((1,), (1,))) for a, b in zip(v, g)]
        slot_of = lax.broadcasted_iota(jnp.int32, s[0].shape, 0) // BLOCK
        p, p16, ds16 = [], [], []
        for u, unit in enumerate(units):
            kept = jnp.where(slot_of < unit[3], s[u], NEG_FILL)
            e = jnp.exp(kept - jnp.max(kept, axis=0, keepdims=True))
            p.append(e * (1.0 / jnp.sum(e, axis=0, keepdims=True)))
            p16.append(p[u].astype(BF16))
        for u in range(len(units)):
            delta = jnp.sum(p[u] * dp[u], axis=0, keepdims=True)
            ds16.append((p[u] * (dp[u] - delta)).astype(BF16))
        for u, (rows, _, home, _, lane) in enumerate(units):
            att_ref[home, lane] = dot(p16[u], v[u], ((0,), (0,))).astype(BF16)
            grads_ref[0, rows, lane] = (dot(ds16[u], k[u], ((0,), (0,))) * scale).astype(BF16)
        for u, (_, at, _, _, lane) in enumerate(units):
            dk = dot(ds16[u], q[u], ((1,), (0,)))
            dv = dot(p16[u], g[u], ((1,), (0,)))
            for i, a in enumerate(at):
                part = slice(i * BLOCK, (i + 1) * BLOCK)
                dk_ref[a, lane] += dk[part]
                dv_ref[a, lane] += dv[part]
        return carry

    lax.fori_loop(0, row_blocks // ROWS, some_rows, 0)
    stores = [pltpu.make_async_copy(grads_ref.at[c], grads_out.at[c], out_sems.at[c]) for c in range(3)]
    stores[0].start()
    grads_ref[1] = (dk_ref[...] * scale).astype(BF16)
    stores[1].start()
    grads_ref[2] = dv_ref[...].astype(BF16)
    stores[2].start()

    def part(i):
        cols = kept_ref.shape[2]
        at = pl.ds(pl.multiple_of(place_ref[i] * cols, cols), cols)
        return sum(dot(grads_ref[c, :tok], w_held[c, at], ((1,), (1,))) for c in range(3))

    n_sent, n_kept = sent_ref.shape[0], kept_ref.shape[0]
    for i in range(n_sent):
        sent_ref[i] = part(i).astype(BF16)
    for i in range(n_kept):
        kept_ref[i] = part(n_sent + i)
    for copy in stores:
        copy.wait()


def attention(cols, count, home, places, n_kept, late, piece, qkv_parts, g_parts, g_places, w_qkv, tok, mp_cols):
    tokens = sum(p.shape[0] for p in g_parts)
    width = g_parts[0].shape[1]
    n_qkv, n_g = len(qkv_parts), len(g_parts)
    late_counts = [len(group) for group in late]
    late = [p for group in late for p in group]
    n_late, late_rows = len(late), sum(p.shape[0] for p in late)
    n_sent = places.shape[0] - n_kept
    return pl.pallas_call(
        functools.partial(attention_kernel, n_qkv, g_places, late_counts, piece, tok),
        out_shape=(
            jax.ShapeDtypeStruct((3, tokens, width), BF16),
            jax.ShapeDtypeStruct((tokens, width), BF16),
            jax.ShapeDtypeStruct((n_sent, tok, mp_cols), BF16),
            jax.ShapeDtypeStruct((n_kept, tok, mp_cols), F32),
        ),
        in_specs=[SMEM] * 4 + [ANY] * (n_late + n_qkv + n_g + 1),
        out_specs=(ANY, VMEM, VMEM, VMEM),
        scratch_shapes=[
            pltpu.VMEM((3, tokens, width), BF16),
            pltpu.VMEM((tokens, width), BF16),
            pltpu.VMEM((tokens, width), F32),
            pltpu.VMEM((tokens, width), F32),
            pltpu.VMEM((3, tokens, width), BF16),
            pltpu.VMEM(w_qkv.shape, BF16),
            pltpu.VMEM((late_rows, late[0].shape[1]), BF16),
            pltpu.SemaphoreType.DMA((n_qkv,)),
            pltpu.SemaphoreType.DMA((tokens // tok,)),
            pltpu.SemaphoreType.DMA((3 * SPLIT,)),
            pltpu.SemaphoreType.DMA((3,)),
            pltpu.SemaphoreType.DMA((late_rows // piece,)),
        ],
        compiler_params=pltpu.CompilerParams(vmem_limit_bytes=60 * MIB),
        cost_estimate=pl.CostEstimate(flops=10**10, bytes_accessed=30 * MIB, transcendentals=0),
        name="attention",
    )(cols, count, home, places, *late, *qkv_parts, *g_parts, w_qkv)


def weight_grad_kernel(counts, piece, chunk_ref, *refs):
    n = sum(counts)
    parts, (grads_ref, out_ref, held, cols_held, sems, cols_sems) = refs[:n], refs[n:]
    rows = held.shape[1] // SPLIT
    cols = cols_held.shape[1]
    here = pl.ds(pl.multiple_of(chunk_ref[0] * cols, cols), cols)
    groups = cut([p.at[:, here] for p in parts], counts)
    loads = load_groups(groups, piece, cols_held, cols_sems)
    grad_loads = []
    for c in range(3):
        for i in range(SPLIT):
            at = pl.ds(i * rows, rows)
            grad_loads.append(pltpu.make_async_copy(grads_ref.at[c, at], held.at[c, at], sems.at[c * SPLIT + i]))
    for load in loads + grad_loads:
        load.start()
    for load in loads:
        load.wait()
    turned = cols_held[...].T
    for c in range(3):
        for load in grad_loads[c * SPLIT : (c + 1) * SPLIT]:
            load.wait()
        out_ref[c] = dot(turned, held[c], ((1,), (0,))).astype(BF16)


def weight_grad(chunk, groups, piece, grads, cols):
    counts = [len(g) for g in groups]
    token_parts = [p for g in groups for p in g]
    n = len(token_parts)
    _, tokens, heads = grads.shape
    return pl.pallas_call(
        functools.partial(weight_grad_kernel, counts, piece),
        in_specs=[SMEM] + [ANY] * (n + 1),
        out_specs=VMEM,
        out_shape=jax.ShapeDtypeStruct((3, cols, heads), BF16),
        scratch_shapes=[
            pltpu.VMEM(grads.shape, BF16),
            pltpu.VMEM((tokens, cols), BF16),
            pltpu.SemaphoreType.DMA((3 * SPLIT,)),
            pltpu.SemaphoreType.DMA((tokens // piece,)),
        ],
        compiler_params=pltpu.CompilerParams(vmem_limit_bytes=60 * MIB),
        cost_estimate=pl.CostEstimate(
            flops=6 * tokens * cols * heads, bytes_accessed=6 * tokens * heads, transcendentals=0
        ),
        name="weight_grad",
    )(chunk, *token_parts, grads)


def local(sizes, tokens_in, w_qkv, w_out, grad_y, block_cols, block_count):
    nz, nx, ny, nc = sizes
    mesh_size = dict(z=nz, x=nx, y=ny, c=nc)
    chunks, pieces = nz * nx, ny * nc
    tok, width = tokens_in.shape
    piece = tok // pieces
    out_cols = width // chunks
    blocks = tok // BLOCK
    y, c = lax.axis_index("y"), lax.axis_index("c")
    chunk = lax.axis_index("z") * nx + lax.axis_index("x")
    quarter = y * nc + c
    quarter_block = quarter * blocks // pieces

    def swap(a, axis, k):
        n = mesh_size[axis]
        return lax.ppermute(a, axis, [(i, i ^ k) for i in range(n)])

    def my_piece(a, k):
        return lax.dynamic_slice_in_dim(a, (quarter ^ k) * piece, piece, 0)

    def after(a, *done):
        return lax.optimization_barrier((a, done))[0]

    batches = [[1, 2], [4, 3], [i for k in range(3, nz) for i in (2 * k, 2 * k - 1)] + [2 * nz - 1]]
    order = [0] + [k for batch in batches for k in batch]
    g_own, g_sent, y_sent = cotangent(quarter, chunk, grad_y, w_out, pieces, chunks)

    def along_z(held, start, k):
        low = k & -k
        held[2 * k] = swap(start if k == low else held[2 * (k ^ low)], "z", low)

    own = my_piece(tokens_in, 0)
    got = {}
    for k in range(1, nz):
        along_z(got, own, k)
    got[1] = swap(own, "x", 1)
    got[3] = swap(after(got[2], got[1], g_own), "x", 1)
    last_x = got[3]
    for k in range(2, nz):
        got[2 * k + 1] = last_x = swap(after(got[2 * k], last_x), "x", 1)

    g_x = swap(after(g_sent, last_x), "x", 1)
    g_z = {}
    for k in range(1, nz):
        low = k & -k
        g_z[k] = swap(after(g_sent, got[4]) if k == low else g_z[k ^ low], "z", low)
    g_far = [g_z[k] for k in range(1, nz)]
    g_far.append(swap(after(join(g_far), g_x), "x", 1))
    g_parts = [g_own, g_x] + g_far
    places = [[0], [1]] + [[2 * k] for k in range(1, nz)] + [[2 * k + 1 for k in range(1, nz)]]
    g_places = [[order.index(k) for k in part] for part in places]

    groups, behind, qkv_parts = [[tokens_in]], [], []
    for at, batch in enumerate(batches):
        mine = join([got[k] for k in batch])
        ys = [mine] + [swap(after(mine, *behind), "y", i) for i in range(1, ny)]
        behind = ys[1:]
        parts = []
        for i, a in enumerate(ys):
            core = after(a, *ys[1:], *(qkv_parts if at == 2 else [])) if i == 0 else a
            parts += [a] + [swap(core, "c", j) for j in range(1, nc)]
        groups.append(parts)
        if at == 0:
            qkv_parts = [project(groups, piece, w_qkv)]
    late = groups[2:]

    y_sent = after(y_sent, *g_far)
    y_all = lax.all_to_all(y_sent, ("z", "x"), 0, 0, tiled=True).reshape(chunks * tok, out_cols)

    held = jnp.repeat(jnp.array(order, jnp.int32), blocks)
    inner = jnp.tile(jnp.arange(blocks, dtype=jnp.int32), chunks)
    number = jnp.arange(chunks * blocks, dtype=jnp.int32)

    def flip(k):
        return jnp.where(k == 0, 0, quarter_block)

    block_at = (held ^ chunk) * blocks + (inner ^ flip(held))
    pick = block_at[:, None] == number[None, :]
    cols = jnp.sum(jnp.where(pick[:, :, None], block_cols[None], 0), axis=1)
    count = jnp.sum(jnp.where(pick, block_count[None], 0), axis=1)
    cols = jnp.sum(jnp.where(cols[:, :, None] == block_at[None, None, :], number[None, None, :], 0), axis=2)
    home = (held ^ chunk) * blocks + inner

    by_y = y ^ jnp.arange(ny, dtype=jnp.int32)
    places = jnp.concatenate([by_y * nc + (c ^ j) for j in range(1, nc)] + [by_y * nc + c])
    grads, att, sent, half = attention(
        cols, count, home, places, ny, late, piece, qkv_parts, g_parts, g_places, w_qkv, tok, width // pieces
    )
    grad_out = dot(att, y_all, ((0,), (0,))).astype(BF16)
    half = after(half, grad_out)
    for j in range(1, nc):
        half = half + swap(sent[(j - 1) * ny : j * ny], "c", j).astype(F32)
    grad_x = half[0]
    for k in range(1, ny):
        grad_x = grad_x + swap(half[k].astype(BF16), "y", k).astype(F32)

    grad_qkv = weight_grad(chunk.reshape(1), groups, piece, after(grads, half), out_cols)
    return (grad_x.astype(BF16), grad_qkv, grad_out)


def solution(mesh):
    chunks, pieces = mesh.shape["blk"], mesh.shape["mp"]
    sizes = (chunks // 2, 2, pieces // 2, 2)
    fine = Mesh(mesh.devices.reshape(sizes), ("z", "x", "y", "c"))
    blk, mp = ("z", "x"), ("y", "c")
    in_specs = (P(blk, None), P(None, None, mp), P(mp, None), P(blk, None), P(), P())
    out_specs = (P(blk, mp), P(None, blk, mp), P(mp, blk))
    return jax.shard_map(
        functools.partial(local, sizes), mesh=fine, in_specs=in_specs, out_specs=out_specs, check_vma=False
    )
```

```python
import functools
import math

import jax
import jax.numpy as jnp
from jax import lax
from jax.experimental import pallas as pl
from jax.experimental.pallas import tpu as pltpu
from jax.sharding import Mesh
from jax.sharding import PartitionSpec as P

HEAD = 128
BLOCK = 128
NEG_FILL = -1e30
BF16 = jnp.bfloat16
F32 = jnp.float32
MIB = 2**20

VMEM = pl.BlockSpec(memory_space=pltpu.VMEM)
SMEM = pl.BlockSpec(memory_space=pltpu.SMEM)
ANY = pl.BlockSpec(memory_space=pl.ANY)


def dot(a, b, dims):
    return lax.dot_general(a, b, (dims, ((), ())), preferred_element_type=F32)


def load_rows(parts, held, sems):
    copies, at = [], 0
    for i, part in enumerate(parts):
        rows = part.shape[-2]
        to = held.at[:, pl.ds(at, rows)] if len(part.shape) == 3 else held.at[pl.ds(at, rows)]
        copies.append(pltpu.make_async_copy(part, to, sems.at[i]))
        at += rows
    return copies


SPLIT = 4
ROWS = 2


def load_pieces(parts, piece, held, sems):
    copies, n = [], len(parts)
    for i, part in enumerate(parts):
        for j in range(part.shape[0] // piece):
            at = j * n + i
            copies.append(
                pltpu.make_async_copy(
                    part.at[pl.ds(j * piece, piece)], held.at[pl.ds(at * piece, piece)], sems.at[at]
                )
            )
    return copies


def load_weights(w_ref, w_held, sems):
    copies = []
    rows = w_ref.shape[1] // SPLIT
    for c in range(3):
        for i in range(SPLIT):
            at = pl.ds(i * rows, rows)
            copies.append(pltpu.make_async_copy(w_ref.at[c, at], w_held.at[c, at], sems.at[c * SPLIT + i]))
    return copies


def load_groups(groups, piece, held, sems):
    copies, at = [], 0
    for group in groups:
        size = piece if len(group) > 1 else group[0].shape[0]
        rows = sum(p.shape[0] for p in group)
        to = held.at[pl.ds(at, rows)]
        copies += load_pieces(group, size, to, sems.at[pl.ds(at // piece, rows // size)])
        at += rows
    return copies


def join_kernel(*refs):
    at = 0
    for part in refs[:-1]:
        refs[-1][at : at + part.shape[0]] = part[...]
        at += part.shape[0]


def join(parts):
    rows = sum(p.shape[0] for p in parts)
    cols = parts[0].shape[1]
    return pl.pallas_call(
        join_kernel,
        out_shape=jax.ShapeDtypeStruct((rows, cols), parts[0].dtype),
        in_specs=[VMEM] * len(parts),
        out_specs=VMEM,
        cost_estimate=pl.CostEstimate(flops=0, bytes_accessed=4 * rows * cols, transcendentals=0),
        name="join",
    )(*parts)


def cut(parts, counts):
    groups, at = [], 0
    for n in counts:
        groups.append(parts[at : at + n])
        at += n
    return groups


def project_kernel(counts, piece, tok, *refs):
    n = sum(counts)
    parts, (w_ref, qkv_ref, held, sems) = refs[:n], refs[n:]

    @pl.when(pl.program_id(0) == 0)
    def _():
        copies = load_groups(cut(parts, counts), piece, held, sems)
        for copy in copies:
            copy.start()
        for copy in copies:
            copy.wait()

    for i in range(0, held.shape[0], tok):
        qkv_ref[0, i : i + tok] = dot(held[i : i + tok], w_ref[0], ((1,), (0,))).astype(BF16)


def project(groups, piece, w_qkv):
    counts = [len(g) for g in groups]
    parts = [p for g in groups for p in g]
    rows = sum(p.shape[0] for p in parts)
    tok = groups[0][0].shape[0]
    _, width, heads = w_qkv.shape
    n = len(parts)
    return pl.pallas_call(
        functools.partial(project_kernel, counts, piece, tok),
        grid=(3,),
        out_shape=jax.ShapeDtypeStruct((3, rows, heads), BF16),
        in_specs=[ANY] * n + [pl.BlockSpec((1, width, heads), lambda c: (c, 0, 0))],
        out_specs=pl.BlockSpec((1, rows, heads), lambda c: (c, 0, 0)),
        scratch_shapes=[pltpu.VMEM((rows, width), BF16), pltpu.SemaphoreType.DMA((rows // piece,))],
        compiler_params=pltpu.CompilerParams(vmem_limit_bytes=32 * MIB),
        cost_estimate=pl.CostEstimate(
            flops=6 * rows * width * heads, bytes_accessed=2 * (3 * heads * (width + rows) + rows * width), transcendentals=0
        ),
        name="project",
    )(*parts, w_qkv)


def cotangent_kernel(pieces, at_ref, grad_y_ref, w_ref, own_ref, sent_ref, cols_ref):
    quarter, chunk = at_ref[0], at_ref[1]
    chunks, tok, cols = cols_ref.shape
    piece = tok // pieces
    own_ref[...] = dot(grad_y_ref[...], w_ref[...], ((1,), (1,))).astype(BF16)
    for i in range(pieces):
        source = pl.ds(pl.multiple_of((quarter ^ i) * piece, piece), piece)
        to = slice(i * piece, (i + 1) * piece)
        sent_ref[to] = own_ref[source]
        for d in range(chunks):
            cols_ref[d, to] = grad_y_ref[source, d * cols : (d + 1) * cols]
    here = pl.ds(pl.multiple_of(chunk * cols, cols), cols)
    cols_ref[chunk] = grad_y_ref[:, here]


def cotangent(quarter, chunk, grad_y, w_out, pieces, chunks):
    tok, width = grad_y.shape
    heads = w_out.shape[0]
    return pl.pallas_call(
        functools.partial(cotangent_kernel, pieces),
        out_shape=(
            jax.ShapeDtypeStruct((tok, heads), BF16),
            jax.ShapeDtypeStruct((tok, heads), BF16),
            jax.ShapeDtypeStruct((chunks, tok, width // chunks), BF16),
        ),
        in_specs=[SMEM, VMEM, VMEM],
        out_specs=(VMEM, VMEM, VMEM),
        compiler_params=pltpu.CompilerParams(vmem_limit_bytes=60 * MIB),
        cost_estimate=pl.CostEstimate(
            flops=2 * tok * width * heads, bytes_accessed=2 * width * (2 * tok + heads), transcendentals=0
        ),
        name="cotangent",
    )(jnp.stack([quarter, chunk]), grad_y, w_out)


def attention_kernel(n_qkv, g_places, late_counts, piece, tok, cols_ref, count_ref, home_ref, place_ref, *refs):
    n_late = sum(late_counts)
    refs, late = refs[n_late:], refs[:n_late]
    n_g = len(g_places)
    qkv_parts, g_parts = refs[:n_qkv], refs[n_qkv : n_qkv + n_g]
    (w_ref, grads_out, att_ref, sent_ref, kept_ref, qkv_ref, g_ref, dk_ref, dv_ref, grads_ref, w_held, held) = refs[n_qkv + n_g : -5]
    qkv_sems, g_sems, w_sems, out_sems, late_sems = refs[-5:]
    row_blocks, slots = cols_ref.shape
    heads = g_ref.shape[1] // HEAD
    scale = 1.0 / math.sqrt(HEAD)
    copies = load_rows(qkv_parts, qkv_ref, qkv_sems)
    for part, places in zip(g_parts, g_places):
        for i, at in enumerate(places):
            to = g_ref.at[pl.ds(at * tok, tok)]
            copies.append(pltpu.make_async_copy(part.at[pl.ds(i * tok, tok)], to, g_sems.at[at]))
    weights = load_weights(w_ref, w_held, w_sems)
    late_copies = load_groups(cut(late, late_counts), piece, held, late_sems)
    for copy in late_copies + weights[:SPLIT]:
        copy.start()
    dk_ref[...] = jnp.zeros_like(dk_ref)
    dv_ref[...] = jnp.zeros_like(dv_ref)
    for copy in late_copies:
        copy.wait()
    for copy in weights[SPLIT:] + copies:
        copy.start()
    first = qkv_ref.shape[1] - held.shape[0]
    for c in range(3):
        for copy in weights[c * SPLIT : (c + 1) * SPLIT]:
            copy.wait()
        for i in range(0, held.shape[0], tok):
            qkv_ref[c, first + i : first + i + tok] = dot(held[i : i + tok], w_held[c], ((1,), (0,))).astype(BF16)
    for copy in copies:
        copy.wait()

    def some_rows(step, carry):
        units = []
        for i in range(ROWS):
            r = step * ROWS + i
            rows = pl.ds(pl.multiple_of(r * BLOCK, BLOCK), BLOCK)
            at = [pl.ds(pl.multiple_of(cols_ref[r, s] * BLOCK, BLOCK), BLOCK) for s in range(slots)]
            home = pl.ds(pl.multiple_of(home_ref[r] * BLOCK, BLOCK), BLOCK)
            for h in range(heads):
                units.append((rows, at, home, count_ref[r], slice(h * HEAD, (h + 1) * HEAD)))
        q = [qkv_ref[0, rows, lane] for rows, _, _, _, lane in units]
        g = [g_ref[rows, lane] for rows, _, _, _, lane in units]
        k = [jnp.concatenate([qkv_ref[1, a, lane] for a in at], axis=0) for _, at, _, _, lane in units]
        v = [jnp.concatenate([qkv_ref[2, a, lane] for a in at], axis=0) for _, at, _, _, lane in units]
        s = [dot(a, b, ((1,), (1,))) * scale for a, b in zip(k, q)]
        dp = [dot(a, b, ((1,), (1,))) for a, b in zip(v, g)]
        slot_of = lax.broadcasted_iota(jnp.int32, s[0].shape, 0) // BLOCK
        p, p16, ds16 = [], [], []
        for u, unit in enumerate(units):
            kept = jnp.where(slot_of < unit[3], s[u], NEG_FILL)
            e = jnp.exp(kept - jnp.max(kept, axis=0, keepdims=True))
            p.append(e * (1.0 / jnp.sum(e, axis=0, keepdims=True)))
            p16.append(p[u].astype(BF16))
        for u in range(len(units)):
            delta = jnp.sum(p[u] * dp[u], axis=0, keepdims=True)
            ds16.append((p[u] * (dp[u] - delta)).astype(BF16))
        for u, (rows, _, home, _, lane) in enumerate(units):
            att_ref[home, lane] = dot(p16[u], v[u], ((0,), (0,))).astype(BF16)
            grads_ref[0, rows, lane] = (dot(ds16[u], k[u], ((0,), (0,))) * scale).astype(BF16)
        for u, (_, at, _, _, lane) in enumerate(units):
            dk = dot(ds16[u], q[u], ((1,), (0,)))
            dv = dot(p16[u], g[u], ((1,), (0,)))
            for i, a in enumerate(at):
                part = slice(i * BLOCK, (i + 1) * BLOCK)
                dk_ref[a, lane] += dk[part]
                dv_ref[a, lane] += dv[part]
        return carry

    lax.fori_loop(0, row_blocks // ROWS, some_rows, 0)
    stores = [pltpu.make_async_copy(grads_ref.at[c], grads_out.at[c], out_sems.at[c]) for c in range(3)]
    stores[0].start()
    grads_ref[1] = (dk_ref[...] * scale).astype(BF16)
    stores[1].start()
    grads_ref[2] = dv_ref[...].astype(BF16)
    stores[2].start()

    def part(i):
        cols = kept_ref.shape[2]
        at = pl.ds(pl.multiple_of(place_ref[i] * cols, cols), cols)
        return sum(dot(grads_ref[c, :tok], w_held[c, at], ((1,), (1,))) for c in range(3))

    n_sent, n_kept = sent_ref.shape[0], kept_ref.shape[0]
    for i in range(n_sent):
        sent_ref[i] = part(i).astype(BF16)
    for i in range(n_kept):
        kept_ref[i] = part(n_sent + i)
    for copy in stores:
        copy.wait()


def attention(cols, count, home, places, n_kept, late, piece, qkv_parts, g_parts, g_places, w_qkv, tok, mp_cols):
    tokens = sum(p.shape[0] for p in g_parts)
    width = g_parts[0].shape[1]
    n_qkv, n_g = len(qkv_parts), len(g_parts)
    late_counts = [len(group) for group in late]
    late = [p for group in late for p in group]
    n_late, late_rows = len(late), sum(p.shape[0] for p in late)
    n_sent = places.shape[0] - n_kept
    return pl.pallas_call(
        functools.partial(attention_kernel, n_qkv, g_places, late_counts, piece, tok),
        out_shape=(
            jax.ShapeDtypeStruct((3, tokens, width), BF16),
            jax.ShapeDtypeStruct((tokens, width), BF16),
            jax.ShapeDtypeStruct((n_sent, tok, mp_cols), BF16),
            jax.ShapeDtypeStruct((n_kept, tok, mp_cols), F32),
        ),
        in_specs=[SMEM] * 4 + [ANY] * (n_late + n_qkv + n_g + 1),
        out_specs=(ANY, VMEM, VMEM, VMEM),
        scratch_shapes=[
            pltpu.VMEM((3, tokens, width), BF16),
            pltpu.VMEM((tokens, width), BF16),
            pltpu.VMEM((tokens, width), F32),
            pltpu.VMEM((tokens, width), F32),
            pltpu.VMEM((3, tokens, width), BF16),
            pltpu.VMEM(w_qkv.shape, BF16),
            pltpu.VMEM((late_rows, late[0].shape[1]), BF16),
            pltpu.SemaphoreType.DMA((n_qkv,)),
            pltpu.SemaphoreType.DMA((tokens // tok,)),
            pltpu.SemaphoreType.DMA((3 * SPLIT,)),
            pltpu.SemaphoreType.DMA((3,)),
            pltpu.SemaphoreType.DMA((late_rows // piece,)),
        ],
        compiler_params=pltpu.CompilerParams(vmem_limit_bytes=60 * MIB),
        cost_estimate=pl.CostEstimate(flops=10**10, bytes_accessed=30 * MIB, transcendentals=0),
        name="attention",
    )(cols, count, home, places, *late, *qkv_parts, *g_parts, w_qkv)


def weight_grad_kernel(counts, piece, chunk_ref, *refs):
    n = sum(counts)
    parts, (grads_ref, out_ref, held, cols_held, sems, cols_sems) = refs[:n], refs[n:]
    rows = held.shape[1] // SPLIT
    cols = cols_held.shape[1]
    here = pl.ds(pl.multiple_of(chunk_ref[0] * cols, cols), cols)
    groups = cut([p.at[:, here] for p in parts], counts)
    loads = load_groups(groups, piece, cols_held, cols_sems)
    grad_loads = []
    for c in range(3):
        for i in range(SPLIT):
            at = pl.ds(i * rows, rows)
            grad_loads.append(pltpu.make_async_copy(grads_ref.at[c, at], held.at[c, at], sems.at[c * SPLIT + i]))
    for load in loads + grad_loads:
        load.start()
    for load in loads:
        load.wait()
    turned = cols_held[...].T
    for c in range(3):
        for load in grad_loads[c * SPLIT : (c + 1) * SPLIT]:
            load.wait()
        out_ref[c] = dot(turned, held[c], ((1,), (0,))).astype(BF16)


def weight_grad(chunk, groups, piece, grads, cols):
    counts = [len(g) for g in groups]
    token_parts = [p for g in groups for p in g]
    n = len(token_parts)
    _, tokens, heads = grads.shape
    return pl.pallas_call(
        functools.partial(weight_grad_kernel, counts, piece),
        in_specs=[SMEM] + [ANY] * (n + 1),
        out_specs=VMEM,
        out_shape=jax.ShapeDtypeStruct((3, cols, heads), BF16),
        scratch_shapes=[
            pltpu.VMEM(grads.shape, BF16),
            pltpu.VMEM((tokens, cols), BF16),
            pltpu.SemaphoreType.DMA((3 * SPLIT,)),
            pltpu.SemaphoreType.DMA((tokens // piece,)),
        ],
        compiler_params=pltpu.CompilerParams(vmem_limit_bytes=60 * MIB),
        cost_estimate=pl.CostEstimate(
            flops=6 * tokens * cols * heads, bytes_accessed=6 * tokens * heads, transcendentals=0
        ),
        name="weight_grad",
    )(chunk, *token_parts, grads)


def local(sizes, tokens_in, w_qkv, w_out, grad_y, block_cols, block_count):
    nz, nx, ny, nc = sizes
    mesh_size = dict(z=nz, x=nx, y=ny, c=nc)
    chunks, pieces = nz * nx, ny * nc
    tok, width = tokens_in.shape
    piece = tok // pieces
    out_cols = width // chunks
    blocks = tok // BLOCK
    y, c = lax.axis_index("y"), lax.axis_index("c")
    chunk = lax.axis_index("z") * nx + lax.axis_index("x")
    quarter = y * nc + c
    quarter_block = quarter * blocks // pieces

    def swap(a, axis, k):
        n = mesh_size[axis]
        return lax.ppermute(a, axis, [(i, i ^ k) for i in range(n)])

    def my_piece(a, k):
        return lax.dynamic_slice_in_dim(a, (quarter ^ k) * piece, piece, 0)

    def after(a, *done):
        return lax.optimization_barrier((a, done))[0]

    batches = [[1, 2], [4, 3], [i for k in range(3, nz) for i in (2 * k, 2 * k - 1)] + [2 * nz - 1]]
    order = [0] + [k for batch in batches for k in batch]
    g_own, g_sent, y_sent = cotangent(quarter, chunk, grad_y, w_out, pieces, chunks)

    def along_z(held, start, k):
        low = k & -k
        held[2 * k] = swap(start if k == low else held[2 * (k ^ low)], "z", low)

    own = my_piece(tokens_in, 0)
    got = {}
    for k in range(1, nz):
        along_z(got, own, k)
    got[1] = swap(own, "x", 1)
    got[3] = swap(after(got[2], got[1], g_own), "x", 1)
    last_x = got[3]
    for k in range(2, nz):
        got[2 * k + 1] = last_x = swap(after(got[2 * k], last_x), "x", 1)

    g_x = swap(after(g_sent, last_x), "x", 1)
    g_z = {}
    for k in range(1, nz):
        low = k & -k
        g_z[k] = swap(after(g_sent, got[4]) if k == low else g_z[k ^ low], "z", low)
    g_far = [g_z[k] for k in range(1, nz)]
    g_far.append(swap(after(join(g_far), g_x), "x", 1))
    g_parts = [g_own, g_x] + g_far
    places = [[0], [1]] + [[2 * k] for k in range(1, nz)] + [[2 * k + 1 for k in range(1, nz)]]
    g_places = [[order.index(k) for k in part] for part in places]

    groups, behind, qkv_parts = [[tokens_in]], [], []
    for at, batch in enumerate(batches):
        mine = join([got[k] for k in batch])
        ys = [mine] + [swap(after(mine, *behind), "y", i) for i in range(1, ny)]
        behind = ys[1:]
        parts = []
        for i, a in enumerate(ys):
            core = after(a, *ys[1:], *(qkv_parts if at == 2 else [])) if i == 0 else a
            parts += [a] + [swap(core, "c", j) for j in range(1, nc)]
        groups.append(parts)
        if at == 0:
            qkv_parts = [project(groups, piece, w_qkv)]
    late = groups[2:]

    y_sent = after(y_sent, *g_far)
    y_all = lax.all_to_all(y_sent, ("z", "x"), 0, 0, tiled=True).reshape(chunks * tok, out_cols)

    held = jnp.repeat(jnp.array(order, jnp.int32), blocks)
    inner = jnp.tile(jnp.arange(blocks, dtype=jnp.int32), chunks)
    number = jnp.arange(chunks * blocks, dtype=jnp.int32)

    def flip(k):
        return jnp.where(k == 0, 0, quarter_block)

    block_at = (held ^ chunk) * blocks + (inner ^ flip(held))
    pick = block_at[:, None] == number[None, :]
    cols = jnp.sum(jnp.where(pick[:, :, None], block_cols[None], 0), axis=1)
    count = jnp.sum(jnp.where(pick, block_count[None], 0), axis=1)
    cols = jnp.sum(jnp.where(cols[:, :, None] == block_at[None, None, :], number[None, None, :], 0), axis=2)
    home = (held ^ chunk) * blocks + inner

    by_y = y ^ jnp.arange(ny, dtype=jnp.int32)
    places = jnp.concatenate([by_y * nc + (c ^ j) for j in range(1, nc)] + [by_y * nc + c])
    grads, att, sent, half = attention(
        cols, count, home, places, ny, late, piece, qkv_parts, g_parts, g_places, w_qkv, tok, width // pieces
    )
    grad_out = dot(att, y_all, ((0,), (0,))).astype(BF16)
    half = after(half, grad_out)
    for j in range(1, nc):
        half = half + swap(sent[(j - 1) * ny : j * ny], "c", j).astype(F32)
    grad_x = half[0]
    for k in range(1, ny):
        grad_x = grad_x + swap(half[k].astype(BF16), "y", k).astype(F32)

    grad_qkv = weight_grad(chunk.reshape(1), groups, piece, after(grads, half), out_cols)
    return (grad_x.astype(BF16), grad_qkv, grad_out)


def solution(mesh):
    chunks, pieces = mesh.shape["blk"], mesh.shape["mp"]
    sizes = (chunks // 2, 2, pieces // 2, 2)
    fine = Mesh(mesh.devices.reshape(sizes), ("z", "x", "y", "c"))
    blk, mp = ("z", "x"), ("y", "c")
    in_specs = (P(blk, None), P(None, None, mp), P(mp, None), P(blk, None), P(), P())
    out_specs = (P(blk, mp), P(None, blk, mp), P(mp, blk))
    return jax.shard_map(
        functools.partial(local, sizes), mesh=fine, in_specs=in_specs, out_specs=out_specs, check_vma=False
    )
```
